256 devices in a mesh: seq: 32 (over z, y), batch: 8 (over x, core).
Axes of the slice: x: 4, y: 4, z: 8, core: 2. Of those that a mesh axis runs over, the one named last changes fastest.
Arguments:
- coarse: bfloat16 [8, 2048, 768], P('batch', 'seq'), may hold values from -6 to 6
- skip: bfloat16 [8, 4096, 768], P('batch', 'seq'), may hold values from -6 to 6
- donor: int32 [8, 4096], P('batch', 'seq'), may hold values from 0 to 4095, as said below
- acceptor: int32 [8, 4096], P('batch', 'seq'), may hold values from 0 to 4095, as said below
- conv_weight: bfloat16 [768, 4, 768], P('seq'), may hold values from -0.15625 to 0.15625
- donor_weight: bfloat16 [768, 768], P('seq'), may hold values from -0.21875 to 0.21875
- acceptor_weight: bfloat16 [768, 768], P('seq'), may hold values from -0.21875 to 0.21875
- track_weight: bfloat16 [768, 367], P('seq'), may hold values from -0.21875 to 0.21875
- gain: bfloat16 [768], P('seq'), may hold values from 0.5 to 1.5
- fine_grad: bfloat16 [8, 4096, 768], P('batch', 'seq'), may hold values from -6 to 6
- score_grad: bfloat16 [8, 4096, 367], P('batch', 'seq'), may hold values from -6 to 6
Outputs:
- scores: bfloat16 [8, 4096, 367], P('batch', 'seq')
- coarse_grad: bfloat16 [8, 2048, 768], P('batch', 'seq')
- skip_grad: bfloat16 [8, 4096, 768], P('batch', 'seq')
- conv_grad: float32 [768, 4, 768], P('seq')
- donor_grad: float32 [768, 768], P('seq')
- acceptor_grad: float32 [768, 768], P('seq')
- track_grad: float32 [768, 367], P('seq')
- gain_grad: float32 [768], P('seq')
The draws below stay inside these ranges and needn't reach their ends.
Inputs may be any that keep to these rules, and one draw needn't show every extreme that they name: `donor`: the donors of pairs k * 128 to (k + 1) * 128 - 1 of a sequence lie in positions k * 128 to (k + 1) * 128 - 1. A pair's acceptor lies in the block of 128 positions of its donor or in one of the two blocks beside it. Of the 128 pairs of one block, at most 64 have their acceptors in any one block, and for every block of pairs some block receives exactly 64.
All inputs are finite; a program needn't handle non-finite values.
Results may differ from the reference program's by a relative error of at most 0.029.
Values may be sent and summed in bfloat16 or wider, within the bound.
No kernel may reach another device: no remote copies, remote signals or barrier semaphores. Data moves between devices by JAX's collectives and lax.ppermute only.
A program may use at most 128 MiB of HBM per device.

```python
import jax
import jax.numpy as jnp
from jax import lax

C = 768
TRACKS = 367
POS_DEV = 128
PAIRS_DEV = 128
HALF_DEV = 64
LENGTH = 4096
HALF = 2048
PAIRS = 4096
N_SEQ = 32
N_BATCH = 8


def inside(group_of, block_id):
    owner_block = block_id - 1 + group_of
    return (owner_block >= 0) & (owner_block < N_SEQ)


def pair_sites(key):
    keys_all = jax.random.split(key, 5)
    shape_all = (N_BATCH, N_SEQ, PAIRS_DEV)
    block_id = jnp.broadcast_to(jnp.arange(N_SEQ, dtype=jnp.int32)[None, :, None], shape_all)
    donor_pos = block_id * POS_DEV + jax.random.randint(keys_all[0], shape_all, 0, POS_DEV, dtype=jnp.int32)
    raw_heavy = jnp.broadcast_to(jax.random.randint(keys_all[1], (N_BATCH, N_SEQ, 1), 0, 3, dtype=jnp.int32), shape_all)
    heavy_group = jnp.where(inside(raw_heavy, block_id), raw_heavy, 1)
    ranking = jax.random.randint(keys_all[2], shape_all, 0, 2 ** 19, dtype=jnp.int32) * PAIRS_DEV + jnp.arange(PAIRS_DEV, dtype=jnp.int32)
    order_of = jnp.argsort(ranking, axis=-1)
    rank_of = jnp.argsort(order_of, axis=-1)
    coin_flip = jax.random.randint(keys_all[3], shape_all, 0, 2, dtype=jnp.int32)
    first_alt = (heavy_group + 1) % 3
    second_alt = (heavy_group + 2) % 3
    chosen = jnp.where(coin_flip == 0, first_alt, second_alt)
    fallback = jnp.where(coin_flip == 0, second_alt, first_alt)
    chosen = jnp.where(inside(chosen, block_id), chosen, fallback)
    group_of = jnp.where(rank_of < PAIRS_DEV // 2, heavy_group, chosen)
    acceptor_pos = (block_id - 1 + group_of) * POS_DEV + jax.random.randint(keys_all[4], shape_all, 0, POS_DEV, dtype=jnp.int32)
    return (donor_pos.reshape(N_BATCH, N_SEQ * PAIRS_DEV).astype(jnp.int32), acceptor_pos.reshape(N_BATCH, N_SEQ * PAIRS_DEV).astype(jnp.int32))


def draw_donor(key, part):
    return pair_sites(key)[0]


def draw_acceptor(key, part):
    return pair_sites(key)[1]


def with_spikes(values, key, source, target, blocks, factor):
    owner, partner = [(jnp.arange(values.shape[dim]) // (values.shape[dim] // blocks)).reshape([-1 if axis == dim else 1 for axis in range(values.ndim)]) for dim in (source, target)]
    chosen = jax.random.permutation(key, blocks)[partner]
    strong = (owner == chosen) | (owner == (partner + blocks // 2) % blocks)
    return jnp.where(strong, factor * values, values)


def shard_levels(stream_key, shape, shards, smallest, top_value):
    def one(axis_at, blocks):
        draws = jax.random.uniform(jax.random.fold_in(jax.random.fold_in(stream_key, 6), axis_at), (blocks,), jnp.float32, smallest / len(shards), top_value / len(shards))
        return jnp.repeat(jnp.exp(draws), shape[axis_at] // blocks).reshape((-1,) + (1,) * (len(shape) - axis_at - 1))

    level = one(*shards[0])
    for cut in shards[1:]:
        level = level * one(*cut)
    return level


def centred(own_key, shape, deviation, limit, pieces=(), kind=jnp.bfloat16):
    values = deviation * jax.random.normal(own_key, shape, jnp.float32)
    if pieces:
        values = values * shard_levels(own_key, shape, pieces, -0.22, 0.18)
    return jnp.clip(values, -limit, limit).astype(kind)


def noise_with(key, dims, spread, limit, cuts, heavy, kind=jnp.bfloat16):
    array = spread * jax.random.normal(key, dims, jnp.float32)
    if cuts:
        array = array * shard_levels(key, dims, cuts, -0.22, 0.18)
    return jnp.clip(with_spikes(array, jax.random.fold_in(key, 3), *heavy), -limit, limit).astype(kind)


def setup_inputs(seed: int = 0) -> dict:
    arg_keys = jax.random.split(jax.random.key(seed), 12)
    coarse = noise_with(arg_keys[0], (N_BATCH, HALF, C), 1.0, 6.0, ((0, 8), (1, 32)), (1, 2, 32, 2.75))
    skip = centred(arg_keys[1], (N_BATCH, LENGTH, C), 1.0, 6.0, ((0, 8), (1, 32)))
    donor = draw_donor(jax.random.fold_in(arg_keys[11], 71), 0)
    acceptor = draw_acceptor(jax.random.fold_in(arg_keys[11], 71), 0)
    conv_weight = centred(arg_keys[4], (C, 4, C), (2 * C) ** -0.5, 0.15625, ((0, 32),))
    donor_weight = centred(arg_keys[5], (C, C), C ** -0.5, 0.21875, ((0, 32),))
    acceptor_weight = centred(arg_keys[6], (C, C), C ** -0.5, 0.21875, ((0, 32),))
    track_weight = centred(arg_keys[7], (C, TRACKS), C ** -0.5, 0.21875, ((0, 32),))
    gain = jnp.clip(1.0 + 0.1 * jax.random.normal(arg_keys[8], (C,), jnp.float32), 0.5, 1.5).astype(jnp.bfloat16)
    fine_grad = centred(arg_keys[9], (N_BATCH, LENGTH, C), 1.0, 6.0, ((0, 8), (1, 32)))
    score_grad = centred(arg_keys[10], (N_BATCH, PAIRS, TRACKS), 1.0, 6.0, ((0, 8), (1, 32)))
    return {"coarse": coarse, "skip": skip, "donor": donor, "acceptor": acceptor, "conv_weight": conv_weight, "donor_weight": donor_weight, "acceptor_weight": acceptor_weight, "track_weight": track_weight, "gain": gain, "fine_grad": fine_grad, "score_grad": score_grad}


def matmul(left_rows, right_rows):
    return jnp.dot(left_rows, right_rows, preferred_element_type=jnp.float32)

def outer_sum(left_rows, right_rows):
    return jnp.dot(left_rows.T, right_rows, preferred_element_type=jnp.float32)

def rounded(values):
    return lax.optimization_barrier(values.astype(jnp.bfloat16)).astype(jnp.float32)

def reference(coarse, skip, donor, acceptor, conv_weight, donor_weight, acceptor_weight, track_weight, gain, fine_grad, score_grad):
    channels = gain.shape[0]
    tap_weights = [conv_weight[:, tap_index, :] for tap_index in range(4)]
    gain_f32 = gain.astype(jnp.float32)

    def sequence_step(carry, inputs):
        coarse_rows, skip_rows, donor_pos, acceptor_pos, fine_rows, score_rows = inputs
        zero_row = jnp.zeros((1, channels), coarse_rows.dtype)
        prev_rows = jnp.concatenate([zero_row, coarse_rows[:-1]], 0)
        next_rows = jnp.concatenate([coarse_rows[1:], zero_row], 0)
        even_rows = matmul(coarse_rows, tap_weights[1]) + matmul(prev_rows, tap_weights[3])
        odd_rows = matmul(coarse_rows, tap_weights[2]) + matmul(next_rows, tap_weights[0])
        conv_out = jnp.stack([even_rows, odd_rows], 1).reshape(-1, channels)
        pre_norm = conv_out + skip_rows.astype(jnp.float32)
        inv_rms = lax.rsqrt(lax.optimization_barrier(jnp.mean(pre_norm * pre_norm, -1, keepdims=True)) + 1e-06)
        hidden = (pre_norm * inv_rms * gain_f32).astype(jnp.bfloat16)
        donor_rows = hidden[donor_pos]
        acceptor_rows = hidden[acceptor_pos]
        proj_donor = matmul(donor_rows, donor_weight).astype(jnp.bfloat16)
        proj_acceptor = matmul(acceptor_rows, acceptor_weight).astype(jnp.bfloat16)
        product = (proj_donor.astype(jnp.float32) * proj_acceptor.astype(jnp.float32)).astype(jnp.bfloat16)
        scores = matmul(product, track_weight).astype(jnp.bfloat16)
        grad_product = matmul(score_rows, track_weight.T)
        grad_donor = (grad_product * proj_acceptor.astype(jnp.float32)).astype(jnp.bfloat16)
        grad_acceptor = (grad_product * proj_donor.astype(jnp.float32)).astype(jnp.bfloat16)
        grad_hidden = fine_rows.astype(jnp.float32).at[donor_pos].add(matmul(grad_donor, donor_weight.T))
        grad_hidden = grad_hidden.at[acceptor_pos].add(matmul(grad_acceptor, acceptor_weight.T))
        scaled = grad_hidden * gain_f32
        cubed = inv_rms * inv_rms * inv_rms
        skip_grad = (inv_rms * scaled - pre_norm * cubed * lax.optimization_barrier(jnp.mean(scaled * pre_norm, -1, keepdims=True))).astype(jnp.bfloat16)
        paired = skip_grad.reshape(-1, 2, channels)
        even_grad = paired[:, 0]
        odd_grad = paired[:, 1]
        prev_odd = jnp.concatenate([zero_row, odd_grad[:-1]], 0)
        next_even = jnp.concatenate([even_grad[1:], zero_row], 0)
        coarse_grad = matmul(prev_odd, tap_weights[0].T) + matmul(even_grad, tap_weights[1].T)
        coarse_grad = (coarse_grad + matmul(odd_grad, tap_weights[2].T) + matmul(next_even, tap_weights[3].T)).astype(jnp.bfloat16)
        gain_rows = grad_hidden * pre_norm * inv_rms
        pad_pairs = jnp.zeros((PAIRS_DEV, channels), jnp.bfloat16)
        acc_rows_pad = jnp.concatenate([pad_pairs, acceptor_rows, pad_pairs], 0)
        acc_grads_pad = jnp.concatenate([pad_pairs, grad_acceptor, pad_pairs], 0)
        owner_pad = jnp.concatenate([jnp.full((PAIRS_DEV,), -1, jnp.int32), (acceptor_pos // POS_DEV).astype(jnp.int32), jnp.full((PAIRS_DEV,), -1, jnp.int32)], 0)

        def block_step(block_index, sums):
            block_index = jnp.asarray(block_index, jnp.int32)
            half_start = block_index * HALF_DEV
            pair_start = block_index * PAIRS_DEV
            pos_start = block_index * POS_DEV

            def cut(source, start, count):
                return lax.dynamic_slice_in_dim(source, start, count, 0)
            centre = cut(coarse_rows, half_start, HALF_DEV)
            before = cut(prev_rows, half_start, HALF_DEV)
            after = cut(next_rows, half_start, HALF_DEV)
            even_block = cut(even_grad, half_start, HALF_DEV)
            odd_block = cut(odd_grad, half_start, HALF_DEV)
            conv_part = jnp.stack([outer_sum(after, odd_block), outer_sum(centre, even_block), outer_sum(centre, odd_block), outer_sum(before, even_block)], 1)
            donor_part = outer_sum(cut(donor_rows, pair_start, PAIRS_DEV), cut(grad_donor, pair_start, PAIRS_DEV))
            track_part = outer_sum(cut(product, pair_start, PAIRS_DEV), cut(score_rows, pair_start, PAIRS_DEV))
            near_rows = cut(acc_rows_pad, pair_start, 3 * PAIRS_DEV)
            near_grads = cut(acc_grads_pad, pair_start, 3 * PAIRS_DEV)
            near_owner = cut(owner_pad, pair_start, 3 * PAIRS_DEV)
            keep = (near_owner == block_index).astype(jnp.bfloat16)[:, None]
            acceptor_part = outer_sum(near_rows * keep, near_grads)
            gain_part = lax.optimization_barrier(jnp.sum(cut(gain_rows, pos_start, POS_DEV), 0))
            return (sums[0] + rounded(conv_part), sums[1] + rounded(donor_part), sums[2] + rounded(acceptor_part), sums[3] + rounded(track_part), sums[4] + rounded(gain_part))
        new_carry = lax.fori_loop(0, N_SEQ, block_step, carry)
        return (new_carry, (scores, coarse_grad, skip_grad))
    initial = (jnp.zeros(conv_weight.shape, jnp.float32), jnp.zeros(donor_weight.shape, jnp.float32), jnp.zeros(acceptor_weight.shape, jnp.float32), jnp.zeros(track_weight.shape, jnp.float32), jnp.zeros(gain.shape, jnp.float32))
    sums, stacked = lax.scan(sequence_step, initial, (coarse, skip, donor, acceptor, fine_grad, score_grad))
    rescale = float(N_BATCH * LENGTH) ** (-0.5)
    return (stacked[0], stacked[1], stacked[2], sums[0] * rescale, sums[1] * rescale, sums[2] * rescale, sums[3] * rescale, sums[4] * rescale)
```

```python
import jax
import jax.numpy as jnp
from jax import lax
from jax.sharding import PartitionSpec as P

NZ, NY, NX, NC = 8, 4, 4, 2
AXES = ("seq", "batch")
BF = jnp.bfloat16
F32 = jnp.float32


def linear(z, y, x, c):
    return ((z * NY + y) * NX + x) * NC + c


def route(move):
    pairs = []
    for z in range(NZ):
        for y in range(NY):
            for x in range(NX):
                for c in range(NC):
                    target = move(z, y, x, c)
                    if target is not None:
                        pairs.append((linear(z, y, x, c), linear(*target)))
    return pairs


def send_z(block, step):
    return lax.ppermute(block, AXES, route(lambda z, y, x, c: ((z + step) % NZ, y, x, c)))


def send_y(block, step):
    return lax.ppermute(block, AXES, route(lambda z, y, x, c: (z, (y + step) % NY, x, c)))


def send_x(block, step):
    return lax.ppermute(block, AXES, route(lambda z, y, x, c: (z, y, (x + step) % NX, c)))


def swap_core(block):
    return lax.ppermute(block, AXES, route(lambda z, y, x, c: (z, y, x, 1 - c)))


def send_seq(block, step):
    def move(z, y, x, c):
        place = z * NY + y + step
        if 0 <= place < NZ * NY:
            return (place // NY, place % NY, x, c)
        return None

    return lax.ppermute(block, AXES, route(move))


def rolled(stack, shift, axis):
    count = stack.shape[axis]
    twice = jnp.concatenate([stack, stack], axis)
    return lax.dynamic_slice_in_dim(twice, (count - shift) % count, count, axis)


def gather_along(block, send, count, place, axis):
    pieces = [block] + [send(block, -step) for step in range(1, count)]
    return rolled(jnp.stack(pieces, axis), place, axis)


def scatter_along(stack, send, count, place, axis):
    def part(step):
        index = (place + step) % count
        return lax.dynamic_index_in_dim(stack, index, axis, keepdims=False)

    total = part(0).astype(F32)
    for step in range(1, count):
        total = total + send(part(step), step).astype(F32)
    return total


def mm(left, right):
    return lax.dot_general(left, right, (((1,), (0,)), ((), ())), preferred_element_type=F32)


def mm_nt(left, right):
    return lax.dot_general(left, right, (((1,), (1,)), ((), ())), preferred_element_type=F32)


def mm_tn(left, right):
    return lax.dot_general(left, right, (((0,), (0,)), ((), ())), preferred_element_type=F32)


def local(
    coarse,
    skip,
    donor,
    acceptor,
    conv_weight,
    donor_weight,
    acceptor_weight,
    track_weight,
    gain,
    fine_grad,
    score_grad,
):
    rows_in, _, channels = conv_weight.shape
    half_rows = coarse.shape[1]
    fine_rows = 2 * half_rows
    pairs = donor.shape[1]
    slots = pairs // 2
    tracks = track_weight.shape[1]
    half = channels // 2
    chunk = 256
    seq = lax.axis_index("seq")
    batch = lax.axis_index("batch")
    z, y = seq // NY, seq % NY
    x, c = batch // NC, batch % NC

    own = coarse[0]
    low = send_seq(own[-1:], 1)
    high = send_seq(own[:1], -1)
    padded = jnp.concatenate([low, own, high], 0)

    tap_slice = lax.dynamic_index_in_dim(conv_weight, x, 1, keepdims=False)
    tap_slice = lax.dynamic_slice_in_dim(tap_slice, c * half, half, 1)
    rest = jnp.concatenate(
        [
            donor_weight,
            acceptor_weight,
            track_weight,
            gain[:, None],
            jnp.zeros((rows_in, 8 * chunk - 2 * channels - tracks - 1), BF),
        ],
        1,
    )
    rest_slice = lax.dynamic_slice_in_dim(rest, batch * chunk, chunk, 1)
    both = jnp.concatenate([tap_slice, rest_slice], 1)
    both = gather_along(both, send_z, NZ, z, 0)
    conv_part_w = gather_along(both[:, :, :half], send_y, NY, y, 1).reshape(channels, half)
    rest_mine = gather_along(both[:, :, half:], send_y, NY, y, 1).reshape(channels, chunk)

    def for_tap(tap):
        start = jnp.where(tap == 0, 2, jnp.where(tap == 3, 0, 1))
        return lax.dynamic_slice_in_dim(padded, start, half_rows, 0)

    left_rows = jnp.stack(
        [for_tap(x)] + [send_x(for_tap((x + step) % NX), step) for step in range(1, NX)], 0
    )
    left_rows = jnp.concatenate([left_rows, swap_core(left_rows)], 0).reshape(-1, channels)

    tap_out = mm(left_rows, conv_part_w).astype(BF).reshape(NC, NX, half_rows, half)
    other_half = swap_core(tap_out[1])
    first = jnp.where(c == 0, tap_out[0], other_half)
    second = jnp.where(c == 0, other_half, tap_out[0])
    tap_full = jnp.concatenate([first, second], 2)
    taps = [tap_full[0]] + [send_x(tap_full[step], -step) for step in range(1, NX)]
    sum_same = taps[0].astype(F32) + taps[2].astype(F32)
    sum_other = taps[1].astype(F32) + taps[3].astype(F32)
    x_odd = x % 2 == 1
    conv_out = jnp.concatenate(
        [jnp.where(x_odd, sum_same, sum_other), jnp.where(x_odd, sum_other, sum_same)], 0
    )

    def split_rows(block):
        return jnp.swapaxes(block.reshape(half_rows, 2, channels), 0, 1).reshape(
            fine_rows, channels
        )

    skip_split = split_rows(skip[0])
    fine_split = split_rows(fine_grad[0])

    chunks = jnp.stack([rest_mine] + [send_x(rest_mine, -step) for step in range(1, NX)], 0)
    chunks_other = swap_core(chunks)

    def chunk_at(index):
        place = (index // NC - x) % NX
        mine = lax.dynamic_index_in_dim(chunks, place, 0, keepdims=False)
        other = lax.dynamic_index_in_dim(chunks_other, place, 0, keepdims=False)
        return jnp.where(c == index % NC, mine, other)

    weight_pair = jnp.concatenate([chunk_at(i) for i in range(6)], 1)
    weight_track = jnp.concatenate([chunk_at(i) for i in range(6, 8)], 1)
    gain_row = weight_track[:, tracks].astype(F32)

    positions = lax.broadcasted_iota(jnp.int32, (1, fine_rows), 1)

    def split_place(place):
        return (place % 2) * half_rows + place // 2

    donor_place = split_place(donor[0] - seq * fine_rows)
    donor_hot = (donor_place[:, None] == positions).astype(BF)
    owner = acceptor[0] // fine_rows
    group = owner - seq
    acceptor_place = split_place(acceptor[0] - owner * fine_rows)
    own_hot = ((acceptor_place[:, None] == positions) & (group[:, None] == 0)).astype(BF)
    pair_index = jnp.arange(pairs, dtype=jnp.int32)
    earlier = (pair_index[:, None] < pair_index[None, :]) & (group[:, None] == group[None, :])
    slot_of = jnp.sum(earlier.astype(jnp.int32), 0)
    slot_index = jnp.arange(slots, dtype=jnp.int32)

    def slot_hot(which):
        return (slot_of[None, :] == slot_index[:, None]) & (group[None, :] == which)

    slot_low, slot_high = slot_hot(-1), slot_hot(1)

    def requests(hot):
        return jnp.sum(jnp.where(hot, acceptor_place[None, :] + 1, 0), 1)

    from_high = send_seq(requests(slot_low), -1)
    from_low = send_seq(requests(slot_high), 1)
    hot_from_high = (from_high[:, None] == positions + 1).astype(BF)
    hot_from_low = (from_low[:, None] == positions + 1).astype(BF)
    slot_low, slot_high = slot_low.astype(BF), slot_high.astype(BF)

    pre_norm = conv_out + skip_split.astype(F32)
    inv_rms = lax.rsqrt(jnp.mean(pre_norm * pre_norm, -1, keepdims=True) + 1e-06)
    hidden = (pre_norm * inv_rms * gain_row).astype(BF)

    projected = mm(hidden, weight_pair).astype(BF)
    all_acceptor = projected[:, channels:]
    rows_low = send_seq(mm(hot_from_low, all_acceptor).astype(BF), -1)
    rows_high = send_seq(mm(hot_from_high, all_acceptor).astype(BF), 1)
    proj_donor = mm(donor_hot, projected[:, :channels])
    pick = jnp.concatenate([own_hot, slot_low.T, slot_high.T], 1)
    proj_acceptor = mm(pick, jnp.concatenate([all_acceptor, rows_high, rows_low], 0))

    score_rows = jnp.concatenate(
        [score_grad[0], jnp.zeros((pairs, 2 * chunk - tracks), BF)], 1
    )
    grad_product = mm_nt(score_rows, weight_track)
    product = (proj_donor * proj_acceptor).astype(BF)
    scores = mm(product, weight_track)[:, :tracks].astype(BF)
    grad_donor = (grad_product * proj_acceptor).astype(BF)
    grad_acceptor = (grad_product * proj_donor).astype(BF)
    to_low = mm(slot_low, grad_acceptor).astype(BF)
    to_high = mm(slot_high, grad_acceptor).astype(BF)
    grads_from_high = send_seq(to_low, -1)
    grads_from_low = send_seq(to_high, 1)
    place_donor = mm_tn(donor_hot, grad_donor).astype(BF)
    owner_hot = jnp.concatenate([own_hot, hot_from_high, hot_from_low], 0)
    place_acceptor = mm_tn(
        owner_hot, jnp.concatenate([grad_acceptor, grads_from_high, grads_from_low], 0)
    ).astype(BF)
    grad_hidden = (
        fine_split.astype(F32)
        + mm_nt(place_donor, weight_pair[:, :channels])
        + mm_nt(place_acceptor, weight_pair[:, channels:])
    )
    scaled = grad_hidden * gain_row
    cubed = inv_rms * inv_rms * inv_rms
    skip_rows = (
        inv_rms * scaled - pre_norm * cubed * jnp.mean(scaled * pre_norm, -1, keepdims=True)
    ).astype(BF)
    gain_terms = grad_hidden * pre_norm * inv_rms
    skip_out = jnp.swapaxes(skip_rows.reshape(2, half_rows, channels), 0, 1).reshape(
        fine_rows, channels
    )

    even_grad, odd_grad = skip_rows[:half_rows], skip_rows[half_rows:]

    def grad_for(step):
        return jnp.where((x + step) % 2 == 1, even_grad, odd_grad)

    grads_x = jnp.stack([grad_for(0)] + [send_x(grad_for(step), step) for step in range(1, NX)], 0)
    lower, upper = grads_x[:, :, :half], grads_x[:, :, half:]
    grads_other = swap_core(jnp.where(c == 0, upper, lower))
    tap_grads = jnp.concatenate([jnp.where(c == 0, lower, upper), grads_other], 0)
    tap_grads = tap_grads.reshape(-1, half)
    conv_part = mm_tn(left_rows, tap_grads)

    back = mm_nt(tap_grads, conv_part_w).astype(BF).reshape(NC, NX, half_rows, channels)
    back_sum = (back[0].astype(F32) + swap_core(back[1]).astype(F32)).astype(BF)
    backs = [back_sum[0]] + [send_x(back_sum[step], -step) for step in range(1, NX)]

    def back_tap(tap):
        return sum(
            jnp.where((x + step) % NX == tap, backs[step].astype(F32), 0.0) for step in range(NX)
        )

    tap_zero, tap_three = back_tap(0), back_tap(3)
    halo_low = send_seq(tap_zero[-1:].astype(BF), 1).astype(F32)
    halo_high = send_seq(tap_three[:1].astype(BF), -1).astype(F32)
    coarse_back = (
        back_tap(1)
        + back_tap(2)
        + jnp.concatenate([halo_low, tap_zero[:-1]], 0)
        + jnp.concatenate([tap_three[1:], halo_high], 0)
    ).astype(BF)

    def mine_and_other(block):
        first, second = block[:, 0], block[:, 1]
        return jnp.where(c == 0, first, second), jnp.where(c == 0, second, first)

    place_both = jnp.concatenate([place_donor, place_acceptor], 1).reshape(fine_rows, 3, 2, chunk)
    right_mine = jnp.where(c == 0, place_both[:, :, 0], place_both[:, :, 1])
    right_send = jnp.where(c == 0, place_both[:, :, 1], place_both[:, :, 0])
    right_mine = right_mine.reshape(fine_rows, 3 * chunk)
    right_send = right_send.reshape(fine_rows, 3 * chunk)
    hidden_two = jnp.concatenate([hidden, swap_core(hidden)], 0)
    right_two = jnp.concatenate([right_mine, swap_core(right_send)], 0)
    score_mine = jnp.where(c == 0, score_rows[:, :chunk], score_rows[:, chunk:])
    score_send = jnp.where(c == 0, score_rows[:, chunk:], score_rows[:, :chunk])
    product_two = jnp.concatenate([product, swap_core(product)], 0)
    score_two = jnp.concatenate([score_mine, swap_core(score_send)], 0)
    pair_part = mm_tn(hidden_two, right_two).astype(BF)
    gain_own = jnp.sum(gain_terms, 0, keepdims=True)
    gain_other = swap_core(gain_own.astype(BF)).astype(F32)
    first_row = lax.broadcasted_iota(jnp.int32, (fine_rows, 1), 0) == 0
    gain_rows = (gain_terms + jnp.where(first_row, gain_other, 0.0)).astype(BF)
    column = lax.broadcasted_iota(jnp.int32, (fine_rows, chunk), 1)
    gain_hot = ((column == tracks - chunk) & (c == 1)).astype(BF)
    track_part = (mm_tn(product_two, score_two) + mm_tn(gain_rows, gain_hot)).astype(BF)
    rest_part = jnp.stack(
        [pair_part[:, :chunk], pair_part[:, chunk : 2 * chunk], pair_part[:, 2 * chunk :], track_part],
        0,
    )
    rest_sum = scatter_along(rest_part, send_x, NX, x, 0)

    def over_seq(block):
        block = block.astype(BF).reshape(NZ, NY, rows_in, block.shape[1])
        block = scatter_along(block, send_y, NY, y, 1).astype(BF)
        return scatter_along(block, send_z, NZ, z, 0).astype(BF)

    shares = jnp.concatenate([over_seq(conv_part), over_seq(rest_sum)], 1)
    shares = gather_along(shares, send_x, NX, x, 0)
    shares_other = swap_core(shares)
    low_share = jnp.where(c == 0, shares, shares_other).astype(F32)
    high_share = jnp.where(c == 0, shares_other, shares).astype(F32)
    rescale = float(NX * NC * NZ * NY * fine_rows) ** (-0.5)
    low_share, high_share = low_share * rescale, high_share * rescale
    conv_grad = jnp.stack(
        [
            jnp.concatenate([low_share[tap, :, :half], high_share[tap, :, :half]], 1)
            for tap in range(NX)
        ],
        1,
    )
    rest_grad = jnp.concatenate(
        [
            piece
            for index in range(NX)
            for piece in (low_share[index, :, half:], high_share[index, :, half:])
        ],
        1,
    )
    donor_grad = rest_grad[:, :channels]
    acceptor_grad = rest_grad[:, channels : 2 * channels]
    track_grad = rest_grad[:, 2 * channels : 2 * channels + tracks]
    gain_grad = rest_grad[:, 2 * channels + tracks]
    return (
        scores[None],
        coarse_back[None],
        skip_out[None],
        conv_grad,
        donor_grad,
        acceptor_grad,
        track_grad,
        gain_grad,
    )


def solution(mesh):
    return jax.shard_map(
        local,
        mesh=mesh,
        in_specs=(
            P("batch", "seq", None),
            P("batch", "seq", None),
            P("batch", "seq"),
            P("batch", "seq"),
            P("seq", None, None),
            P("seq", None),
            P("seq", None),
            P("seq", None),
            P("seq"),
            P("batch", "seq", None),
            P("batch", "seq", None),
        ),
        out_specs=(
            P("batch", "seq", None),
            P("batch", "seq", None),
            P("batch", "seq", None),
            P("seq", None, None),
            P("seq", None),
            P("seq", None),
            P("seq", None),
            P("seq"),
        ),
        check_vma=False,
    )
```

```python
import functools

import jax
import jax.numpy as jnp
from jax import lax
from jax.experimental import pallas as pl
from jax.experimental.pallas import tpu as pltpu
from jax.sharding import Mesh
from jax.sharding import PartitionSpec as P

AXES = ("z", "y", "x", "c")
SEQ = ("z", "y")
GROUP = ("x", "c")
BF = jnp.bfloat16
F32 = jnp.float32
CHUNK = 256


def send_seq(block, step):
    count = lax.axis_size(SEQ)
    pairs = [(i, i + step) for i in range(count) if 0 <= i + step < count]
    return lax.ppermute(block, SEQ, pairs)


def send_edge(block, steps):
    sizes = [lax.axis_size(axis) for axis in AXES]
    seqs, per = sizes[0] * sizes[1], sizes[2] * sizes[3]
    pairs = []
    for source in range(seqs):
        for member in range(per):
            step = steps[member // sizes[3]]
            if step and 0 <= source + step < seqs:
                pairs.append((source * per + member, (source + step) * per + member))
    return lax.ppermute(block, AXES, pairs)


def send_x(block, step):
    count = lax.axis_size("x")
    return lax.ppermute(block, "x", [(i, (i + step) % count) for i in range(count)])


def swap_core(block):
    return lax.ppermute(block, "c", [(0, 1), (1, 0)])


def mm(left, right):
    return lax.dot_general(left, right, (((1,), (0,)), ((), ())), preferred_element_type=F32)


def mm_nt(left, right):
    return lax.dot_general(left, right, (((1,), (1,)), ((), ())), preferred_element_type=F32)


def mm_tn(left, right):
    return lax.dot_general(left, right, (((0,), (0,)), ((), ())), preferred_element_type=F32)


def call(body, shapes, *operands, scratch=(), scalars=0):
    vmem = pl.BlockSpec(memory_space=pltpu.VMEM)
    smem = pl.BlockSpec(memory_space=pltpu.SMEM)
    return pl.pallas_call(
        body,
        out_shape=[jax.ShapeDtypeStruct(shape, kind) for shape, kind in shapes],
        in_specs=[smem] * scalars + [vmem] * (len(operands) - scalars),
        out_specs=[vmem] * len(shapes),
        scratch_shapes=[pltpu.VMEM(shape, kind) for shape, kind in scratch],
        compiler_params=pltpu.CompilerParams(vmem_limit_bytes=16 * 1024 * 1024),
    )(*operands)


def split_hot(rows, transposed):
    row = lax.broadcasted_iota(jnp.int32, (rows, rows), 0)
    column = lax.broadcasted_iota(jnp.int32, (rows, rows), 1)
    if transposed:
        row, column = column, row
    hot = (row % 2) * (rows // 2) + row // 2 == column
    return jnp.where(hot, 1.0, 0.0).astype(BF)


def inverse(pre):
    return lax.rsqrt(jnp.mean(pre * pre, -1, keepdims=True) + 1e-06)


def start_body(
    place_ref, conv_ref, donor_ref, acceptor_ref, track_ref, gain_ref, coarse_ref, out_ref, own_ref
):
    x, c = place_ref[0], place_ref[1]
    half = out_ref.shape[1] - CHUNK
    half_rows = coarse_ref.shape[0]
    own_ref[:half_rows] = coarse_ref[...]
    own_ref[half_rows:] = jnp.zeros_like(own_ref[half_rows:])
    depth = out_ref.shape[0]
    for member in range(8):
        tap, part = member // 2, member % 2

        @pl.when((x == tap) & (c == part))
        def _():
            out_ref[:, :half] = conv_ref[:, tap, part * half : (part + 1) * half]
            if member == 7:
                tracks = track_ref.shape[1]
                pad = jnp.zeros((depth, 2 * CHUNK - tracks - 1), BF)
                out_ref[:, half:] = jnp.concatenate([track_ref[:, CHUNK:], gain_ref[...], pad], 1)
            else:
                source = (donor_ref, acceptor_ref, track_ref)[member // 3]
                first = (member % 3) * CHUNK
                out_ref[:, half:] = source[:, first : first + CHUNK]


def norm_body(taps_ref, skip_ref, pre_ref, unit_ref):
    def tap(index):
        return taps_ref[index].astype(F32)

    half_rows = taps_ref.shape[1]
    half = taps_ref.shape[2]
    skip = mm(split_hot(2 * half_rows, True), skip_ref[...])
    pre_ref[:half_rows, :half] = tap(2) + tap(6) + skip[:half_rows, :half]
    pre_ref[:half_rows, half:] = tap(3) + tap(7) + skip[:half_rows, half:]
    pre_ref[half_rows:, :half] = tap(4) + tap(0) + skip[half_rows:, :half]
    pre_ref[half_rows:, half:] = tap(5) + tap(1) + skip[half_rows:, half:]
    pre = pre_ref[...]
    unit_ref[...] = (pre * inverse(pre)).astype(BF)


def one_hot(mask):
    return jnp.where(mask, 1.0, 0.0).astype(BF)


def pair_body(
    pre_ref, chunks_ref, low_ref, high_ref, donor_ref, place_ref, group_ref, group_row_ref, score_ref,
    hidden_ref, product_ref, to_low_ref, to_high_ref, place_donor_ref, own_ref, gain_ref,
    grad_donor_ref, grad_acceptor_ref,
):
    pre = pre_ref[...]
    rows = pre.shape[0]
    slots = rows // 2
    gains = mm_nt(gain_hot(score_ref.shape[1] - CHUNK), chunks_ref[7])
    gain = gains[:1]
    gain_ref[...] = gains
    hidden = (pre * inverse(pre) * gain).astype(BF)
    hidden_ref[...] = hidden
    near = [(ref[...].astype(F32) * gain).astype(BF) for ref in (low_ref, high_ref)]
    lanes = lax.broadcasted_iota(jnp.int32, (rows, rows), 1)
    group = group_ref[...]
    at_place = place_ref[...] == lanes
    donor_hot = one_hot(donor_ref[...] == lanes)
    own_hot = one_hot(at_place & (group == 0))
    pick = jnp.concatenate(
        [own_hot, one_hot(at_place & (group == -1)), one_hot(at_place & (group == 1))], 1
    )
    donor_rows = mm(donor_hot, hidden).astype(BF)
    acceptor_rows = mm(pick, jnp.concatenate([hidden] + near, 0)).astype(BF)
    score = score_ref[...]
    tracks = score.shape[1]
    for index in range(3):
        cols = slice(index * CHUNK, (index + 1) * CHUNK)
        proj_donor = mm(donor_rows, chunks_ref[index]).astype(BF).astype(F32)
        proj_acceptor = mm(acceptor_rows, chunks_ref[3 + index]).astype(BF).astype(F32)
        grad = mm_nt(score[:, :CHUNK], chunks_ref[6, cols]) + mm_nt(
            score[:, CHUNK:], chunks_ref[7, cols, : tracks - CHUNK]
        )
        product_ref[:, cols] = (proj_donor * proj_acceptor).astype(BF)
        grad_donor_ref[:, cols] = (grad * proj_acceptor).astype(BF)
        grad_acceptor_ref[:, cols] = (grad * proj_donor).astype(BF)
    grad_acceptor = grad_acceptor_ref[...]
    before = lax.broadcasted_iota(jnp.int32, (rows, rows), 0) > lanes
    same = group == group_row_ref[...]
    slot_of = jnp.sum(jnp.where(before & same, 1.0, 0.0), 1, keepdims=True).astype(jnp.int32)
    slot_lanes = lax.broadcasted_iota(jnp.int32, (rows, slots), 1)
    numbers = (place_ref[...] + 1).astype(F32)
    first = lax.broadcasted_iota(jnp.int32, (16, rows), 0) == 0
    for which, ref in ((-1, to_low_ref), (1, to_high_ref)):
        hot = (slot_of == slot_lanes) & (group == which)
        ref[:slots] = mm_tn(one_hot(hot), grad_acceptor).astype(BF)
        index_row = jnp.sum(jnp.where(hot, numbers, 0.0), 0, keepdims=True)
        index_row = jnp.concatenate([index_row, jnp.zeros((1, rows - slots), F32)], 1)
        ref[slots:] = jnp.zeros_like(ref[slots:])
        ref[slots:, :rows] = jnp.where(first, index_row, 0.0).astype(BF)
    place_donor_ref[...] = mm_tn(donor_hot, grad_donor_ref[...]).astype(BF)
    own_ref[...] = mm_tn(own_hot, grad_acceptor)


def gain_hot(column):
    return one_hot(lax.broadcasted_iota(jnp.int32, (16, CHUNK), 1) == column)


def base_body(product_ref, chunks_ref, place_ref, fine_ref, scores_ref, base_ref):
    rows = fine_ref.shape[0]
    product = product_ref[...]
    tracks = scores_ref.shape[1]
    scores_ref[:, :CHUNK] = mm(product, chunks_ref[6]).astype(BF)
    scores_ref[:, CHUNK:] = mm(product, chunks_ref[7])[:, : tracks - CHUNK].astype(BF)
    place = place_ref[...]
    total = mm(split_hot(rows, True), fine_ref[...])
    for index in range(3):
        total = total + mm_nt(place[:, index * CHUNK : (index + 1) * CHUNK], chunks_ref[index])
    base_ref[...] = total


def skip_body(
    base_ref, own_ref, chunks_ref, low_ref, high_ref, pre_ref, gain_ref, place_ref, score_ref,
    skip_ref, out_ref,
):
    rows = pre_ref.shape[0]
    half_rows = rows // 2
    channels = pre_ref.shape[1]
    half = channels // 2
    acceptor = own_ref[...]
    numbers = lax.broadcasted_iota(jnp.int32, (rows, half_rows), 0) + 1
    for ref in (low_ref, high_ref):
        asked = ref[half_rows:, :rows].astype(F32)[:1, :half_rows].astype(jnp.int32)
        acceptor = acceptor + mm(one_hot(numbers == asked), ref[:half_rows])
    acceptor = acceptor.astype(BF)
    grad = base_ref[...]
    for index in range(3):
        grad = grad + mm_nt(
            acceptor[:, index * CHUNK : (index + 1) * CHUNK], chunks_ref[3 + index]
        )
    pre = pre_ref[...]
    inv = inverse(pre)
    scaled = grad * gain_ref[:1]
    mean = jnp.mean(scaled * pre, -1, keepdims=True)
    skip = (inv * scaled - pre * (inv * inv * inv) * mean).astype(BF)
    skip_ref[...] = mm(split_hot(rows, False), skip).astype(BF)
    gains = jnp.sum(grad * pre * inv, 0, keepdims=True)
    row = lax.broadcasted_iota(jnp.int32, (half_rows, 128), 0)
    gain_block = jnp.zeros((half_rows, 128), F32)
    for index in range(channels // 128):
        gain_block = jnp.where(row == index, gains[:, index * 128 : (index + 1) * 128], gain_block)
    for index in range(8):
        start = half_rows if (index // 2) % 2 == 0 else 0
        part = (index % 2) * half
        out_ref[index, :, :half] = skip[start : start + half_rows, part : part + half]
        if index == 7:
            tracks = score_ref.shape[1]
            wide = jnp.zeros((rows, 2 * CHUNK - tracks), BF)
            block = jnp.concatenate([score_ref[:, CHUNK:], wide], 1)
        elif index == 6:
            block = score_ref[:, :CHUNK]
        elif index < 3:
            block = place_ref[:, index * CHUNK : (index + 1) * CHUNK]
        else:
            block = acceptor[:, (index - 3) * CHUNK : (index - 2) * CHUNK]
        out_ref[index, :, half : half + CHUNK] = block[:half_rows]
        out_ref[index, :, half + CHUNK :] = block[half_rows:]
    out_ref[7, :, half + 128 : half + CHUNK] = gain_block.astype(BF)


def partial_body(place_ref, left_ref, near_ref, far_ref, grads_ref, out_ref, rows_ref, right_ref):
    x, c = place_ref[0], place_ref[1]
    members, half_rows, _ = grads_ref.shape
    half = left_ref.shape[1] // 2
    rows = 2 * half_rows
    for member in range(members):
        span = pl.ds(member * rows, rows)
        step = lax.rem(x - member // 2 + 4, 4)

        @pl.when(c == member % 2)
        def _():
            rows_ref[span] = near_ref[step]

        @pl.when(c != member % 2)
        def _():
            rows_ref[span] = far_ref[step]

        right_ref[member * rows : member * rows + half_rows] = grads_ref[member, :, half : half + CHUNK]
        right_ref[member * rows + half_rows : (member + 1) * rows] = grads_ref[member, :, half + CHUNK :]
    taps = grads_ref[:, :, :half].reshape(members * half_rows, half)
    wide_y, wide_z, depth, _ = out_ref.shape

    def store(values, columns):
        for z in range(wide_z):
            for y in range(wide_y):
                row = (z * wide_y + y) * depth
                out_ref[y, z, :, columns] = values[row : row + depth].astype(BF)

    store(mm_tn(left_ref[...], taps), slice(0, half))
    rest = mm_tn(rows_ref[...], right_ref[...])
    total = jnp.sum(grads_ref[:, :16, half + 128 : half + CHUNK].astype(F32), 0)
    row = lax.broadcasted_iota(jnp.int32, (128, 128), 0)
    lane = lax.broadcasted_iota(jnp.int32, (128, 128), 1)
    ones = jnp.ones((128, 128), BF)
    gains = [
        mm(jnp.where(row == lane, total[index : index + 1], 0.0).astype(BF), ones)
        for index in range(2 * half // 128)
    ]
    store(rest[:, :128], slice(half, half + 128))
    gain_last = (x == 3) & (c == 1)
    store(
        jnp.where(gain_last, jnp.concatenate(gains, 0), rest[:, 128:]),
        slice(half + 128, half + CHUNK),
    )


def final_body(rescale, shares_ref, conv_ref, donor_ref, acceptor_ref, track_ref, gain_ref):
    half = conv_ref.shape[2] // 2
    tracks = track_ref.shape[1]
    for member in range(8):
        values = shares_ref[member].astype(F32) * rescale
        tap, part = member // 2, member % 2
        conv_ref[:, tap, part * half : (part + 1) * half] = values[:, :half]
        if member == 7:
            track_ref[:, CHUNK:] = values[:, half : half + tracks - CHUNK]
            gain_ref[...] = values[:, half + CHUNK // 2 : half + CHUNK // 2 + 1]
        else:
            target = (donor_ref, acceptor_ref, track_ref)[member // 3]
            first = (member % 3) * CHUNK
            target[:, first : first + CHUNK] = values[:, half:]


def local(
    coarse,
    skip,
    donor,
    acceptor,
    conv_weight,
    donor_weight,
    acceptor_weight,
    track_weight,
    gain,
    fine_grad,
    score_grad,
):
    rows_in, _, channels = conv_weight.shape
    half_rows = coarse.shape[1]
    fine_rows = 2 * half_rows
    pairs = donor.shape[1]
    slots = pairs // 2
    tracks = track_weight.shape[1]
    half = channels // 2
    nz, ny, nx, nc = (lax.axis_size(axis) for axis in AXES)
    group_size = nx * nc
    seqs = nz * ny
    seq = lax.axis_index(SEQ)
    batch = lax.axis_index(GROUP)
    x, c = lax.axis_index("x"), lax.axis_index("c")

    place = jnp.stack([x, c])
    both, own = call(
        start_body,
        [((rows_in, half + CHUNK), BF), ((half_rows + 32, channels), BF)],
        place, conv_weight, donor_weight, acceptor_weight, track_weight, gain[:, None], coarse[0],
        scalars=1,
    )
    both = jnp.broadcast_to(both[None], (nz, rows_in, half + CHUNK))
    both = lax.all_to_all(both, "z", 0, 0, tiled=True)

    def over_y(block):
        block = jnp.broadcast_to(block[None], (ny,) + block.shape)
        block = lax.all_to_all(block, "y", 0, 0, tiled=True)
        return jnp.swapaxes(block, 0, 1).reshape(channels, block.shape[-1])

    gathered = over_y(both)
    conv_w = gathered[:, :half]
    chunks = lax.all_gather(gathered[:, half:], GROUP, axis=0)

    left_all = lax.all_gather(own, GROUP, axis=0)[:, :half_rows]
    edge = jnp.where(x == 0, left_all[:, 0], left_all[:, half_rows - 1])
    edge = send_edge(edge, (-1, 0, 0, 1))[:, None]
    wide_rows = jnp.concatenate([edge, left_all, edge], 1)
    first_row = jnp.where(x == 0, 2, jnp.where(x == nx - 1, 0, 1))
    left_rows = lax.dynamic_slice_in_dim(wide_rows, first_row, half_rows, 1)
    left_rows = left_rows.reshape(-1, channels)

    tap_out = mm(left_rows, conv_w).astype(BF).reshape(group_size, half_rows, half)
    taps = lax.all_to_all(tap_out, GROUP, 0, 0, tiled=True)

    def split_place(place):
        return (place % 2) * half_rows + place // 2

    donor_place = split_place(donor[0] - seq * fine_rows)[:, None]
    owner = acceptor[0] // fine_rows
    group = owner - seq
    acceptor_place = split_place(acceptor[0] - owner * fine_rows)[:, None]

    fine_shape = (fine_rows, channels)
    sent_shape = (slots + 16, channels)
    pre_norm, unit = call(norm_body, [(fine_shape, F32), (fine_shape, BF)], taps, skip[0])
    near_high = send_seq(unit, -1)
    near_low = send_seq(unit, 1)
    hidden, product, to_low, to_high, place_donor, own_grads, gain_rows = call(
        pair_body,
        [(fine_shape, BF), (fine_shape, BF), (sent_shape, BF), (sent_shape, BF), (fine_shape, BF)]
        + [(fine_shape, F32), ((16, channels), F32)],
        pre_norm, chunks, near_low, near_high, donor_place, acceptor_place, group[:, None], group[None, :],
        score_grad[0],
        scratch=[(fine_shape, BF), (fine_shape, BF)],
    )
    grads_high = send_seq(to_low, -1)
    grads_low = send_seq(to_high, 1)
    is_track = [(x + step) % nx == nx - 1 for step in range(nx)]
    left_near = [jnp.where(last, product, hidden) for last in is_track]
    left_near = jnp.stack(
        left_near[:1] + [send_x(left_near[step], step) for step in range(1, nx)], 0
    )
    scores, base = call(
        base_body, [((pairs, tracks), BF), (fine_shape, F32)], product, chunks, place_donor, fine_grad[0]
    )
    skip_out, outgoing = call(
        skip_body,
        [(fine_shape, BF), ((group_size, half_rows, half + 2 * CHUNK), BF)],
        base, own_grads, chunks, grads_low, grads_high, pre_norm, gain_rows, place_donor, score_grad[0],
    )
    outgoing, left_near = lax.optimization_barrier((outgoing, left_near))
    left_far = swap_core(left_near)
    grads = lax.all_to_all(outgoing, GROUP, 0, 0, tiled=True)
    tap_grads = grads[:, :, :half]
    grad_edge = jnp.where(x == 0, tap_grads[:, half_rows - 1], tap_grads[:, 0])
    grad_edge = send_edge(grad_edge, (1, 0, 0, -1))[:, None]
    (partials,) = call(
        partial_body,
        [((ny, nz, rows_in, half + CHUNK), BF)],
        place, left_rows, left_near, left_far, grads,
        scratch=[((group_size * fine_rows, channels), BF), ((group_size * fine_rows, CHUNK), BF)],
        scalars=1,
    )
    wide_grads = jnp.concatenate([grad_edge, tap_grads, grad_edge], 1)
    first_grad = jnp.where(x == 0, 0, jnp.where(x == nx - 1, 2, 1))
    moved = lax.dynamic_slice_in_dim(wide_grads, first_grad, half_rows, 1).reshape(-1, half)
    back = mm_nt(moved, conv_w).astype(BF).reshape(group_size, half_rows, channels)
    partials, back = lax.optimization_barrier((partials, back))
    coarse_back = lax.psum_scatter(back, GROUP, scatter_dimension=0, tiled=True)
    shares = lax.all_to_all(partials, "y", 0, 0, tiled=True)
    shares = jnp.sum(shares.astype(F32), 0).astype(BF)
    shares = lax.all_to_all(shares, "z", 0, 0, tiled=True)
    shares, coarse_back = lax.optimization_barrier((shares, coarse_back))
    shares = jnp.sum(shares.astype(F32), 0).astype(BF)
    shares = jnp.broadcast_to(shares[None], (group_size,) + shares.shape)
    shares = lax.all_to_all(shares, GROUP, 0, 0, tiled=True)

    rescale = float(group_size * seqs * fine_rows) ** (-0.5)
    conv_grad, donor_grad, acceptor_grad, track_grad, gain_grad = call(
        functools.partial(final_body, rescale),
        [((rows_in, nx, channels), F32), ((rows_in, channels), F32), ((rows_in, channels), F32)]
        + [((rows_in, tracks), F32), ((rows_in, 1), F32)],
        shares,
    )
    gain_grad = gain_grad[:, 0]
    return (
        scores[None],
        coarse_back,
        skip_out[None],
        conv_grad,
        donor_grad,
        acceptor_grad,
        track_grad,
        gain_grad,
    )


def solution(mesh):
    wide = Mesh(mesh.devices.reshape(8, 4, 4, 2), AXES)
    return jax.shard_map(
        local,
        mesh=wide,
        in_specs=(
            P(GROUP, SEQ, None),
            P(GROUP, SEQ, None),
            P(GROUP, SEQ),
            P(GROUP, SEQ),
            P(SEQ, None, None),
            P(SEQ, None),
            P(SEQ, None),
            P(SEQ, None),
            P(SEQ),
            P(GROUP, SEQ, None),
            P(GROUP, SEQ, None),
        ),
        out_specs=(
            P(GROUP, SEQ, None),
            P(GROUP, SEQ, None),
            P(GROUP, SEQ, None),
            P(SEQ, None, None),
            P(SEQ, None),
            P(SEQ, None),
            P(SEQ, None),
            P(SEQ),
        ),
        check_vma=False,
    )
```

```python
import functools

import jax
import jax.numpy as jnp
from jax import lax
from jax.experimental import pallas as pl
from jax.experimental.pallas import tpu as pltpu
from jax.sharding import Mesh
from jax.sharding import PartitionSpec as P

AXES = ("z", "y", "x", "c")
SEQ = ("z", "y")
GROUP = ("x", "c")
BF = jnp.bfloat16
F32 = jnp.float32
CHUNK = 256


def send_seq(block, step):
    count = lax.axis_size(SEQ)
    pairs = [(i, i + step) for i in range(count) if 0 <= i + step < count]
    return lax.ppermute(block, SEQ, pairs)


def send_edge(block, steps):
    sizes = [lax.axis_size(axis) for axis in AXES]
    seqs, per = sizes[0] * sizes[1], sizes[2] * sizes[3]
    pairs = []
    for source in range(seqs):
        for member in range(per):
            step = steps[member // sizes[3]]
            if step and 0 <= source + step < seqs:
                pairs.append((source * per + member, (source + step) * per + member))
    return lax.ppermute(block, AXES, pairs)


def send_x(block, step):
    count = lax.axis_size("x")
    return lax.ppermute(block, "x", [(i, (i + step) % count) for i in range(count)])


def swap_core(block):
    return lax.ppermute(block, "c", [(0, 1), (1, 0)])


def mm(left, right):
    return lax.dot_general(left, right, (((1,), (0,)), ((), ())), preferred_element_type=F32)


def mm_nt(left, right):
    return lax.dot_general(left, right, (((1,), (1,)), ((), ())), preferred_element_type=F32)


def mm_tn(left, right):
    return lax.dot_general(left, right, (((0,), (0,)), ((), ())), preferred_element_type=F32)


def call(body, shapes, *operands, scratch=(), mib=16):
    vmem = pl.BlockSpec(memory_space=pltpu.VMEM)
    return pl.pallas_call(
        body,
        out_shape=[jax.ShapeDtypeStruct(shape, kind) for shape, kind in shapes],
        in_specs=[vmem] * len(operands),
        out_specs=[vmem] * len(shapes),
        scratch_shapes=list(scratch),
        compiler_params=pltpu.CompilerParams(vmem_limit_bytes=mib * 1024 * 1024),
    )(*operands)


def split_hot(rows, transposed):
    row = lax.broadcasted_iota(jnp.int32, (rows, rows), 0)
    column = lax.broadcasted_iota(jnp.int32, (rows, rows), 1)
    if transposed:
        row, column = column, row
    hot = (row % 2) * (rows // 2) + row // 2 == column
    return jnp.where(hot, 1.0, 0.0).astype(BF)


def inverse(pre):
    return lax.rsqrt(jnp.mean(pre * pre, -1, keepdims=True) + 1e-06)


def start_body(
    conv_ref, donor_ref, acceptor_ref, track_ref, gain_ref, coarse_ref, out_ref, own_ref
):
    x, c = lax.axis_index("x"), lax.axis_index("c")
    half = out_ref.shape[2] - CHUNK
    half_rows = coarse_ref.shape[0]
    own_ref[:half_rows] = coarse_ref[...]
    own_ref[half_rows:] = jnp.zeros_like(own_ref[half_rows:])
    copies, depth = out_ref.shape[:2]
    for member in range(8):
        tap, part = member // 2, member % 2

        @pl.when((x == tap) & (c == part))
        def _():
            taps = conv_ref[:, tap, part * half : (part + 1) * half]
            if member == 7:
                tracks = track_ref.shape[1]
                pad = jnp.zeros((depth, 2 * CHUNK - tracks - 1), BF)
                row = lax.broadcasted_iota(jnp.int32, (depth, depth), 0)
                lane = lax.broadcasted_iota(jnp.int32, (depth, depth), 1)
                gains = jnp.where(row == lane, gain_ref[...].astype(F32), 0.0)
                gains = jnp.sum(gains, 1, keepdims=True).astype(BF)
                rest = jnp.concatenate([track_ref[:, CHUNK:], gains, pad], 1)
            else:
                source = (donor_ref, acceptor_ref, track_ref)[member // 3]
                first = (member % 3) * CHUNK
                rest = source[:, first : first + CHUNK]
            for index in range(copies):
                out_ref[index, :, :half] = taps
                out_ref[index, :, half:] = rest


def shift_rows(x, down, up, load, edge_ref, rows_ref, members):
    depth = rows_ref.shape[0] // members
    for member in range(members):
        span = slice(member * depth, (member + 1) * depth)

        @pl.when(x == up)
        def _():
            block = load(member).astype(F32)
            edge = edge_ref[member : member + 1].astype(F32)
            rows_ref[span] = jnp.concatenate([block[1:], edge], 0).astype(BF)

        @pl.when(x == down)
        def _():
            block = load(member).astype(F32)
            edge = edge_ref[member : member + 1].astype(F32)
            rows_ref[span] = jnp.concatenate([edge, block[:-1]], 0).astype(BF)

        @pl.when((x != down) & (x != up))
        def _():
            rows_ref[span] = load(member)


def conv_body(both_ref, left_ref, edge_ref, out_ref, weight_ref, rows_ref):
    x = lax.axis_index("x")
    wide_y, wide_z, _, _ = both_ref.shape
    members, half_rows, half = out_ref.shape
    planes = [
        both_ref[y, z, :, :half].astype(F32) for z in range(wide_z) for y in range(wide_y)
    ]
    weight_ref[...] = jnp.concatenate(planes, 0).astype(BF)
    shift_rows(x, 3, 0, lambda member: left_ref[member, :half_rows], edge_ref, rows_ref, members)
    result = mm(rows_ref[...], weight_ref[...]).astype(BF)
    out_ref[...] = result.reshape(members, half_rows, half)


def norm_body(taps_ref, skip_ref, pre_ref, unit_ref):
    def tap(index):
        return taps_ref[index].astype(F32)

    half_rows = taps_ref.shape[1]
    half = taps_ref.shape[2]
    skip = mm(split_hot(2 * half_rows, True), skip_ref[...])
    pre_ref[:half_rows, :half] = tap(2) + tap(6) + skip[:half_rows, :half]
    pre_ref[:half_rows, half:] = tap(3) + tap(7) + skip[:half_rows, half:]
    pre_ref[half_rows:, :half] = tap(4) + tap(0) + skip[half_rows:, :half]
    pre_ref[half_rows:, half:] = tap(5) + tap(1) + skip[half_rows:, half:]
    pre = pre_ref[...]
    unit_ref[...] = (pre * inverse(pre)).astype(BF)


def one_hot(mask):
    return jnp.where(mask, 1.0, 0.0).astype(BF)


def pair_body(
    pre_ref, chunks_ref, low_ref, high_ref, donor_ref, place_ref, group_ref, group_row_ref, score_ref,
    hidden_ref, product_ref, to_low_ref, to_high_ref, place_donor_ref, own_ref, gain_ref,
    grad_donor_ref, grad_acceptor_ref,
):
    pre = pre_ref[...]
    rows = pre.shape[0]
    slots = rows // 2
    gains = mm_nt(gain_hot(score_ref.shape[1] - CHUNK), chunks_ref[7])
    gain = gains[:1]
    gain_ref[...] = gains
    hidden = (pre * inverse(pre) * gain).astype(BF)
    hidden_ref[...] = hidden
    near = [(ref[...].astype(F32) * gain).astype(BF) for ref in (low_ref, high_ref)]
    lanes = lax.broadcasted_iota(jnp.int32, (rows, rows), 1)
    group = group_ref[...]
    at_place = place_ref[...] == lanes
    donor_hot = one_hot(donor_ref[...] == lanes)
    own_hot = one_hot(at_place & (group == 0))
    pick = jnp.concatenate(
        [own_hot, one_hot(at_place & (group == -1)), one_hot(at_place & (group == 1))], 1
    )
    donor_rows = mm(donor_hot, hidden).astype(BF)
    acceptor_rows = mm(pick, jnp.concatenate([hidden] + near, 0)).astype(BF)
    score = score_ref[...]
    tracks = score.shape[1]
    for index in range(3):
        cols = slice(index * CHUNK, (index + 1) * CHUNK)
        proj_donor = mm(donor_rows, chunks_ref[index]).astype(BF).astype(F32)
        proj_acceptor = mm(acceptor_rows, chunks_ref[3 + index]).astype(BF).astype(F32)
        grad = mm_nt(score[:, :CHUNK], chunks_ref[6, cols]) + mm_nt(
            score[:, CHUNK:], chunks_ref[7, cols, : tracks - CHUNK]
        )
        product_ref[:, cols] = (proj_donor * proj_acceptor).astype(BF)
        grad_donor_ref[:, cols] = (grad * proj_acceptor).astype(BF)
        grad_acceptor_ref[:, cols] = (grad * proj_donor).astype(BF)
    grad_acceptor = grad_acceptor_ref[...]
    before = lax.broadcasted_iota(jnp.int32, (rows, rows), 0) > lanes
    same = group == group_row_ref[...]
    slot_of = jnp.sum(jnp.where(before & same, 1.0, 0.0), 1, keepdims=True).astype(jnp.int32)
    slot_lanes = lax.broadcasted_iota(jnp.int32, (rows, slots), 1)
    numbers = (place_ref[...] + 1).astype(F32)
    first = lax.broadcasted_iota(jnp.int32, (16, rows), 0) == 0
    for which, ref in ((-1, to_low_ref), (1, to_high_ref)):
        hot = (slot_of == slot_lanes) & (group == which)
        ref[:slots] = mm_tn(one_hot(hot), grad_acceptor).astype(BF)
        index_row = jnp.sum(jnp.where(hot, numbers, 0.0), 0, keepdims=True)
        index_row = jnp.concatenate([index_row, jnp.zeros((1, rows - slots), F32)], 1)
        ref[slots:] = jnp.zeros_like(ref[slots:])
        ref[slots:, :rows] = jnp.where(first, index_row, 0.0).astype(BF)
    place_donor_ref[...] = mm_tn(donor_hot, grad_donor_ref[...]).astype(BF)
    own_ref[...] = mm_tn(own_hot, grad_acceptor)


def gain_hot(column):
    return one_hot(lax.broadcasted_iota(jnp.int32, (16, CHUNK), 1) == column)


def base_body(product_ref, chunks_ref, place_ref, fine_ref, scores_ref, base_ref):
    rows = fine_ref.shape[0]
    product = product_ref[...]
    tracks = scores_ref.shape[0]
    scores_ref[:CHUNK] = mm(product, chunks_ref[6]).T.astype(BF)
    scores_ref[CHUNK:] = mm(product, chunks_ref[7]).T[: tracks - CHUNK].astype(BF)
    place = place_ref[...]
    total = mm(split_hot(rows, True), fine_ref[...])
    for index in range(3):
        total = total + mm_nt(place[:, index * CHUNK : (index + 1) * CHUNK], chunks_ref[index])
    base_ref[...] = total


def skip_body(
    base_ref, own_ref, chunks_ref, low_ref, high_ref, pre_ref, gain_ref, place_ref, score_ref,
    skip_ref, out_ref,
):
    rows = pre_ref.shape[0]
    half_rows = rows // 2
    channels = pre_ref.shape[1]
    half = channels // 2
    acceptor = own_ref[...]
    numbers = lax.broadcasted_iota(jnp.int32, (rows, half_rows), 0) + 1
    for ref in (low_ref, high_ref):
        asked = ref[half_rows:, :rows].astype(F32)[:1, :half_rows].astype(jnp.int32)
        acceptor = acceptor + mm(one_hot(numbers == asked), ref[:half_rows])
    acceptor = acceptor.astype(BF)
    grad = base_ref[...]
    for index in range(3):
        grad = grad + mm_nt(
            acceptor[:, index * CHUNK : (index + 1) * CHUNK], chunks_ref[3 + index]
        )
    pre = pre_ref[...]
    inv = inverse(pre)
    scaled = grad * gain_ref[:1]
    mean = jnp.mean(scaled * pre, -1, keepdims=True)
    skip = (inv * scaled - pre * (inv * inv * inv) * mean).astype(BF)
    skip_ref[...] = mm(split_hot(rows, False), skip).astype(BF)
    gains = jnp.sum(grad * pre * inv, 0, keepdims=True)
    row = lax.broadcasted_iota(jnp.int32, (half_rows, 128), 0)
    gain_block = jnp.zeros((half_rows, 128), F32)
    for index in range(channels // 128):
        gain_block = jnp.where(row == index, gains[:, index * 128 : (index + 1) * 128], gain_block)
    for index in range(8):
        start = half_rows if (index // 2) % 2 == 0 else 0
        part = (index % 2) * half
        out_ref[index, :, :half] = skip[start : start + half_rows, part : part + half]
        if index == 7:
            tracks = score_ref.shape[1]
            wide = jnp.zeros((rows, 2 * CHUNK - tracks), BF)
            block = jnp.concatenate([score_ref[:, CHUNK:], wide], 1)
        elif index == 6:
            block = score_ref[:, :CHUNK]
        elif index < 3:
            block = place_ref[:, index * CHUNK : (index + 1) * CHUNK]
        else:
            block = acceptor[:, (index - 3) * CHUNK : (index - 2) * CHUNK]
        out_ref[index, :, half : half + CHUNK] = block[:half_rows]
        out_ref[index, :, half + CHUNK :] = block[half_rows:]
    out_ref[7, :, half + 128 : half + CHUNK] = gain_block.astype(BF)


def partial_body(left_ref, near_ref, far_ref, grads_ref, out_ref, rows_ref, right_ref):
    x, c = lax.axis_index("x"), lax.axis_index("c")
    members, half_rows, _ = grads_ref.shape
    half = left_ref.shape[1] // 2
    rows = 2 * half_rows
    for member in range(members):
        span = pl.ds(member * rows, rows)
        step = lax.rem(x - member // 2 + 4, 4)

        @pl.when(c == member % 2)
        def _():
            rows_ref[span] = near_ref[step]

        @pl.when(c != member % 2)
        def _():
            rows_ref[span] = far_ref[step]

        right_ref[member * rows : member * rows + half_rows] = grads_ref[member, :, half : half + CHUNK]
        right_ref[member * rows + half_rows : (member + 1) * rows] = grads_ref[member, :, half + CHUNK :]
    taps = grads_ref[:, :, :half].reshape(members * half_rows, half)
    wide_y, wide_z, depth, _ = out_ref.shape

    def store(values, columns):
        for z in range(wide_z):
            for y in range(wide_y):
                row = (z * wide_y + y) * depth
                out_ref[y, z, :, columns] = values[row : row + depth].astype(BF)

    store(mm_tn(left_ref[...], taps), slice(0, half))
    rest = mm_tn(rows_ref[...], right_ref[...])
    total = jnp.sum(grads_ref[:, :16, half + 128 : half + CHUNK].astype(F32), 0)
    row = lax.broadcasted_iota(jnp.int32, (128, 128), 0)
    lane = lax.broadcasted_iota(jnp.int32, (128, 128), 1)
    ones = jnp.ones((128, 128), BF)
    gains = [
        mm(jnp.where(row == lane, total[index : index + 1], 0.0).astype(BF), ones)
        for index in range(2 * half // 128)
    ]
    store(rest[:, :128], slice(half, half + 128))
    gain_last = (x == 3) & (c == 1)
    store(
        jnp.where(gain_last, jnp.concatenate(gains, 0), rest[:, 128:]),
        slice(half + 128, half + CHUNK),
    )


def back_body(grads_ref, edge_ref, weight_ref, mine_ref, other_ref, rows_ref):
    x, c = lax.axis_index("x"), lax.axis_index("c")
    members, half_rows, _ = grads_ref.shape
    half = weight_ref.shape[1]
    shift_rows(x, 0, 3, lambda member: grads_ref[member, :, :half], edge_ref, rows_ref, members)
    result = mm_nt(rows_ref[...], weight_ref[...]).astype(BF)
    for member in range(members):
        block = result[member * half_rows : (member + 1) * half_rows]
        step = lax.rem(member // 2 - x + 4, 4)

        @pl.when(c == member % 2)
        def _():
            mine_ref[step] = block

        @pl.when(c != member % 2)
        def _():
            other_ref[step] = block


def add_body(left_ref, right_ref, out_ref):
    out_ref[...] = (left_ref[...].astype(F32) + right_ref[...].astype(F32)).astype(BF)


def copies_body(parts_ref, out_ref):
    total = parts_ref[0].astype(F32)
    for index in range(1, parts_ref.shape[0]):
        total = total + parts_ref[index].astype(F32)
    total = total.astype(BF)
    for index in range(out_ref.shape[0]):
        out_ref[index] = total


def final_body(
    rescale, shares_ref, backs_ref, conv_ref, donor_ref, acceptor_ref, track_ref, gain_ref, back_ref
):
    half = conv_ref.shape[2] // 2
    tracks = track_ref.shape[1]
    back = backs_ref[0].astype(F32)
    for member in range(1, backs_ref.shape[0]):
        back = back + backs_ref[member].astype(F32)
    back_ref[...] = back.astype(BF)
    for member in range(8):
        values = shares_ref[member].astype(F32) * rescale
        tap, part = member // 2, member % 2
        conv_ref[:, tap, part * half : (part + 1) * half] = values[:, :half]
        if member == 7:
            track_ref[:, CHUNK:] = values[:, half : half + tracks - CHUNK]
            depth = values.shape[0]
            column = values[:, half + CHUNK // 2 : half + CHUNK // 2 + 1]
            row = lax.broadcasted_iota(jnp.int32, (depth, depth), 0)
            lane = lax.broadcasted_iota(jnp.int32, (depth, depth), 1)
            gain_ref[...] = jnp.sum(jnp.where(row == lane, column, 0.0), 0, keepdims=True)
        else:
            target = (donor_ref, acceptor_ref, track_ref)[member // 3]
            first = (member % 3) * CHUNK
            target[:, first : first + CHUNK] = values[:, half : half + CHUNK]


def local(
    coarse,
    skip,
    donor,
    acceptor,
    conv_weight,
    donor_weight,
    acceptor_weight,
    track_weight,
    gain,
    fine_grad,
    score_grad,
):
    rows_in, _, channels = conv_weight.shape
    half_rows = coarse.shape[1]
    fine_rows = 2 * half_rows
    pairs = donor.shape[1]
    slots = pairs // 2
    tracks = track_weight.shape[1]
    half = channels // 2
    nz, ny, nx, nc = (lax.axis_size(axis) for axis in AXES)
    group_size = nx * nc
    seqs = nz * ny
    seq = lax.axis_index(SEQ)
    batch = lax.axis_index(GROUP)
    x, c = lax.axis_index("x"), lax.axis_index("c")

    both, own = call(
        start_body,
        [((nz, rows_in, half + CHUNK), BF), ((half_rows + 32, channels), BF)],
        conv_weight, donor_weight, acceptor_weight, track_weight, gain[None, :], coarse[0],
        mib=56,
    )
    both = lax.all_to_all(both, "z", 0, 0, tiled=True)

    both = jnp.broadcast_to(both[None], (ny,) + both.shape)
    both = lax.all_to_all(both, "y", 0, 0, tiled=True)
    rest_mine = jnp.swapaxes(both[:, :, :, half:], 0, 1).reshape(channels, CHUNK)

    left_all = lax.all_gather(own, GROUP, axis=0)
    edge = jnp.where(x == 0, left_all[:, 0], left_all[:, half_rows - 1])
    edge = send_edge(edge, (-1, 0, 0, 1))
    tap_out, conv_w, left_rows = call(
        conv_body,
        [((group_size, half_rows, half), BF), ((channels, half), BF)]
        + [((group_size * half_rows, channels), BF)],
        both, left_all, edge,
    )
    rest_mine, tap_out = lax.optimization_barrier((rest_mine, tap_out))
    chunks = lax.all_gather(rest_mine, GROUP, axis=0)
    taps = lax.all_to_all(tap_out, GROUP, 0, 0, tiled=True)

    def split_place(place):
        return (place % 2) * half_rows + place // 2

    donor_place = split_place(donor[0] - seq * fine_rows)[:, None]
    owner = acceptor[0] // fine_rows
    group = owner - seq
    acceptor_place = split_place(acceptor[0] - owner * fine_rows)[:, None]

    fine_shape = (fine_rows, channels)
    sent_shape = (slots + 16, channels)
    pre_norm, unit = call(norm_body, [(fine_shape, F32), (fine_shape, BF)], taps, skip[0])
    near_high = send_seq(unit, -1)
    near_low = send_seq(unit, 1)
    hidden, product, to_low, to_high, place_donor, own_grads, gain_rows = call(
        pair_body,
        [(fine_shape, BF), (fine_shape, BF), (sent_shape, BF), (sent_shape, BF), (fine_shape, BF)]
        + [(fine_shape, F32), ((16, channels), F32)],
        pre_norm, chunks, near_low, near_high, donor_place, acceptor_place, group[:, None], group[None, :],
        score_grad[0],
        scratch=[pltpu.VMEM(fine_shape, BF), pltpu.VMEM(fine_shape, BF)],
    )
    grads_high = send_seq(to_low, -1)
    grads_low = send_seq(to_high, 1)
    is_track = [(x + step) % nx == nx - 1 for step in range(nx)]
    left_near = [jnp.where(last, product, hidden) for last in is_track]
    left_near = jnp.stack(
        left_near[:1] + [send_x(left_near[step], step) for step in range(1, nx)], 0
    )
    scores, base = call(
        base_body, [((tracks, pairs), BF), (fine_shape, F32)], product, chunks, place_donor, fine_grad[0]
    )
    skip_out, outgoing = call(
        skip_body,
        [(fine_shape, BF), ((group_size, half_rows, half + 2 * CHUNK), BF)],
        base, own_grads, chunks, grads_low, grads_high, pre_norm, gain_rows, place_donor, score_grad[0],
    )
    outgoing, left_near = lax.optimization_barrier((outgoing, left_near))
    left_far = swap_core(left_near)
    grads = lax.all_to_all(outgoing, GROUP, 0, 0, tiled=True)
    tap_grads = grads[:, :, :half]
    grad_edge = jnp.where(x == 0, tap_grads[:, half_rows - 1], tap_grads[:, 0])
    grad_edge = send_edge(grad_edge, (1, 0, 0, -1))
    (partials,) = call(
        partial_body,
        [((ny, nz, rows_in, half + CHUNK), BF)],
        left_rows, left_near, left_far, grads,
        scratch=[
            pltpu.VMEM((group_size * fine_rows, channels), BF),
            pltpu.VMEM((group_size * fine_rows, CHUNK), BF),
        ],
    )
    slabs = (nx, half_rows, channels)
    back_mine, back_other = call(
        back_body, [(slabs, BF), (slabs, BF)], grads, grad_edge, conv_w,
        scratch=[pltpu.VMEM((group_size * half_rows, half), BF)],
    )
    (back_sum,) = call(add_body, [(slabs, BF)], back_mine, swap_core(back_other))
    backs = jnp.stack(
        [back_sum[0]] + [send_x(back_sum[step], step) for step in range(1, nx)], 0
    )
    shares = lax.all_to_all(partials, "y", 0, 0, tiled=True)
    shares = jnp.sum(shares.astype(F32), 0).astype(BF)
    shares = lax.all_to_all(shares, "z", 0, 0, tiled=True)
    shares, backs = lax.optimization_barrier((shares, backs))
    (shares,) = call(copies_body, [((group_size, rows_in, half + CHUNK), BF)], shares)
    shares = lax.all_to_all(shares, GROUP, 0, 0, tiled=True)

    rescale = float(group_size * seqs * fine_rows) ** (-0.5)
    conv_grad, donor_grad, acceptor_grad, track_grad, gain_grad, coarse_back = call(
        functools.partial(final_body, rescale),
        [((rows_in, nx, channels), F32), ((rows_in, channels), F32), ((rows_in, channels), F32)]
        + [((rows_in, tracks), F32), ((1, rows_in), F32), ((half_rows, channels), BF)],
        shares, backs,
    )
    gain_grad = gain_grad[0]
    return (
        scores.T[None],
        coarse_back[None],
        skip_out[None],
        conv_grad,
        donor_grad,
        acceptor_grad,
        track_grad,
        gain_grad,
    )


def solution(mesh):
    wide = Mesh(mesh.devices.reshape(8, 4, 4, 2), AXES)
    return jax.shard_map(
        local,
        mesh=wide,
        in_specs=(
            P(GROUP, SEQ, None),
            P(GROUP, SEQ, None),
            P(GROUP, SEQ),
            P(GROUP, SEQ),
            P(SEQ, None, None),
            P(SEQ, None),
            P(SEQ, None),
            P(SEQ, None),
            P(SEQ),
            P(GROUP, SEQ, None),
            P(GROUP, SEQ, None),
        ),
        out_specs=(
            P(GROUP, SEQ, None),
            P(GROUP, SEQ, None),
            P(GROUP, SEQ, None),
            P(SEQ, None, None),
            P(SEQ, None),
            P(SEQ, None),
            P(SEQ, None),
            P(SEQ),
        ),
        check_vma=False,
    )
```

```python
import functools

import jax
import jax.numpy as jnp
from jax import lax
from jax.experimental import pallas as pl
from jax.experimental.pallas import tpu as pltpu
from jax.sharding import Mesh
from jax.sharding import PartitionSpec as P

AXES = ("z", "y", "x", "c")
SEQ = ("z", "y")
GROUP = ("x", "c")
BF = jnp.bfloat16
F32 = jnp.float32
CHUNK = 256


def send_seq(block, step):
    count = lax.axis_size(SEQ)
    pairs = [(i, i + step) for i in range(count) if 0 <= i + step < count]
    return lax.ppermute(block, SEQ, pairs)


def send_edge(block, steps):
    sizes = [lax.axis_size(axis) for axis in AXES]
    seqs, per = sizes[0] * sizes[1], sizes[2] * sizes[3]
    pairs = []
    for source in range(seqs):
        for member in range(per):
            step = steps[member // sizes[3]]
            if step and 0 <= source + step < seqs:
                pairs.append((source * per + member, (source + step) * per + member))
    return lax.ppermute(block, AXES, pairs)


def send_x(block, step):
    count = lax.axis_size("x")
    return lax.ppermute(block, "x", [(i, (i + step) % count) for i in range(count)])


def swap_core(block):
    return lax.ppermute(block, "c", [(0, 1), (1, 0)])


def mm(left, right):
    return lax.dot_general(left, right, (((1,), (0,)), ((), ())), preferred_element_type=F32)


def mm_nt(left, right):
    return lax.dot_general(left, right, (((1,), (1,)), ((), ())), preferred_element_type=F32)


def mm_tn(left, right):
    return lax.dot_general(left, right, (((0,), (0,)), ((), ())), preferred_element_type=F32)


def call(body, shapes, *operands, scratch=(), mib=16):
    vmem = pl.BlockSpec(memory_space=pltpu.VMEM)
    return pl.pallas_call(
        body,
        out_shape=[jax.ShapeDtypeStruct(shape, kind) for shape, kind in shapes],
        in_specs=[vmem] * len(operands),
        out_specs=[vmem] * len(shapes),
        scratch_shapes=list(scratch),
        compiler_params=pltpu.CompilerParams(vmem_limit_bytes=mib * 1024 * 1024),
    )(*operands)


def split_hot(rows, transposed):
    row = lax.broadcasted_iota(jnp.int32, (rows, rows), 0)
    column = lax.broadcasted_iota(jnp.int32, (rows, rows), 1)
    if transposed:
        row, column = column, row
    hot = (row % 2) * (rows // 2) + row // 2 == column
    return jnp.where(hot, 1.0, 0.0).astype(BF)


def inverse(pre):
    return lax.rsqrt(jnp.mean(pre * pre, -1, keepdims=True) + 1e-06)


def start_body(
    conv_ref, donor_ref, acceptor_ref, track_ref, gain_ref, coarse_ref, out_ref, own_ref
):
    x, c = lax.axis_index("x"), lax.axis_index("c")
    half = out_ref.shape[2] - CHUNK
    half_rows = coarse_ref.shape[0]
    own_ref[:half_rows] = coarse_ref[...]
    own_ref[half_rows:] = jnp.zeros_like(own_ref[half_rows:])
    copies, depth = out_ref.shape[:2]
    for member in range(8):
        tap, part = member // 2, member % 2

        @pl.when((x == tap) & (c == part))
        def _():
            taps = conv_ref[:, tap, part * half : (part + 1) * half]
            if member == 7:
                tracks = track_ref.shape[1]
                pad = jnp.zeros((depth, 2 * CHUNK - tracks - 1), BF)
                row = lax.broadcasted_iota(jnp.int32, (depth, depth), 0)
                lane = lax.broadcasted_iota(jnp.int32, (depth, depth), 1)
                gains = jnp.where(row == lane, gain_ref[...].astype(F32), 0.0)
                gains = jnp.sum(gains, 1, keepdims=True).astype(BF)
                rest = jnp.concatenate([track_ref[:, CHUNK:], gains, pad], 1)
            else:
                source = (donor_ref, acceptor_ref, track_ref)[member // 3]
                first = (member % 3) * CHUNK
                rest = source[:, first : first + CHUNK]
            for index in range(copies):
                out_ref[index, :, :half] = taps
                out_ref[index, :, half:] = rest


def shift_rows(x, down, up, load, edge_ref, rows_ref, members):
    depth = rows_ref.shape[0] // members
    for member in range(members):
        span = slice(member * depth, (member + 1) * depth)

        @pl.when(x == up)
        def _():
            block = load(member).astype(F32)
            edge = edge_ref[member : member + 1].astype(F32)
            rows_ref[span] = jnp.concatenate([block[1:], edge], 0).astype(BF)

        @pl.when(x == down)
        def _():
            block = load(member).astype(F32)
            edge = edge_ref[member : member + 1].astype(F32)
            rows_ref[span] = jnp.concatenate([edge, block[:-1]], 0).astype(BF)

        @pl.when((x != down) & (x != up))
        def _():
            rows_ref[span] = load(member)


def conv_body(both_ref, left_ref, edge_ref, out_ref, weight_ref, rows_ref):
    x = lax.axis_index("x")
    wide_y, wide_z, _, _ = both_ref.shape
    members, half_rows, half = out_ref.shape
    planes = [
        both_ref[y, z, :, :half].astype(F32) for z in range(wide_z) for y in range(wide_y)
    ]
    weight_ref[...] = jnp.concatenate(planes, 0).astype(BF)
    shift_rows(x, 3, 0, lambda member: left_ref[member, :half_rows], edge_ref, rows_ref, members)
    result = mm(rows_ref[...], weight_ref[...]).astype(BF)
    out_ref[...] = result.reshape(members, half_rows, half)


def norm_body(taps_ref, skip_ref, pre_ref, unit_ref):
    def tap(index):
        return taps_ref[index].astype(F32)

    half_rows = taps_ref.shape[1]
    half = taps_ref.shape[2]
    skip = mm(split_hot(2 * half_rows, True), skip_ref[...])
    pre_ref[:half_rows, :half] = tap(2) + tap(6) + skip[:half_rows, :half]
    pre_ref[:half_rows, half:] = tap(3) + tap(7) + skip[:half_rows, half:]
    pre_ref[half_rows:, :half] = tap(4) + tap(0) + skip[half_rows:, :half]
    pre_ref[half_rows:, half:] = tap(5) + tap(1) + skip[half_rows:, half:]
    pre = pre_ref[...]
    unit_ref[...] = (pre * inverse(pre)).astype(BF)


def one_hot(mask):
    return jnp.where(mask, 1.0, 0.0).astype(BF)


def pair_body(
    pre_ref, chunks_ref, low_ref, high_ref, donor_ref, place_ref, group_ref, group_row_ref, score_ref,
    hidden_ref, product_ref, to_low_ref, to_high_ref, place_donor_ref, own_ref, gain_ref,
    grad_donor_ref, grad_acceptor_ref,
):
    pre = pre_ref[...]
    rows = pre.shape[0]
    slots = rows // 2
    gains = mm_nt(gain_hot(score_ref.shape[1] - CHUNK), chunks_ref[7])
    gain = gains[:1]
    gain_ref[...] = gains
    hidden = (pre * inverse(pre) * gain).astype(BF)
    hidden_ref[...] = hidden
    near = [(ref[...].astype(F32) * gain).astype(BF) for ref in (low_ref, high_ref)]
    lanes = lax.broadcasted_iota(jnp.int32, (rows, rows), 1)
    group = group_ref[...]
    at_place = place_ref[...] == lanes
    donor_hot = one_hot(donor_ref[...] == lanes)
    own_hot = one_hot(at_place & (group == 0))
    pick = jnp.concatenate(
        [own_hot, one_hot(at_place & (group == -1)), one_hot(at_place & (group == 1))], 1
    )
    donor_rows = mm(donor_hot, hidden).astype(BF)
    acceptor_rows = mm(pick, jnp.concatenate([hidden] + near, 0)).astype(BF)
    score = score_ref[...]
    tracks = score.shape[1]
    for index in range(3):
        cols = slice(index * CHUNK, (index + 1) * CHUNK)
        proj_donor = mm(donor_rows, chunks_ref[index]).astype(BF).astype(F32)
        proj_acceptor = mm(acceptor_rows, chunks_ref[3 + index]).astype(BF).astype(F32)
        grad = mm_nt(score[:, :CHUNK], chunks_ref[6, cols]) + mm_nt(
            score[:, CHUNK:], chunks_ref[7, cols, : tracks - CHUNK]
        )
        product_ref[:, cols] = (proj_donor * proj_acceptor).astype(BF)
        grad_donor_ref[:, cols] = (grad * proj_acceptor).astype(BF)
        grad_acceptor_ref[:, cols] = (grad * proj_donor).astype(BF)
    grad_acceptor = grad_acceptor_ref[...]
    before = lax.broadcasted_iota(jnp.int32, (rows, rows), 0) > lanes
    same = group == group_row_ref[...]
    slot_of = jnp.sum(jnp.where(before & same, 1.0, 0.0), 1, keepdims=True).astype(jnp.int32)
    slot_lanes = lax.broadcasted_iota(jnp.int32, (rows, slots), 1)
    numbers = (place_ref[...] + 1).astype(F32)
    first = lax.broadcasted_iota(jnp.int32, (16, rows), 0) == 0
    for which, ref in ((-1, to_low_ref), (1, to_high_ref)):
        hot = (slot_of == slot_lanes) & (group == which)
        ref[:slots] = mm_tn(one_hot(hot), grad_acceptor).astype(BF)
        index_row = jnp.sum(jnp.where(hot, numbers, 0.0), 0, keepdims=True)
        index_row = jnp.concatenate([index_row, jnp.zeros((1, rows - slots), F32)], 1)
        ref[slots:] = jnp.zeros_like(ref[slots:])
        ref[slots:, :rows] = jnp.where(first, index_row, 0.0).astype(BF)
    place_donor_ref[...] = mm_tn(donor_hot, grad_donor_ref[...]).astype(BF)
    own_ref[...] = mm_tn(own_hot, grad_acceptor)


def gain_hot(column):
    return one_hot(lax.broadcasted_iota(jnp.int32, (16, CHUNK), 1) == column)


def skip_body(
    product_ref, fine_ref, own_ref, chunks_ref, low_ref, high_ref, pre_ref, gain_ref, place_ref, score_ref,
    skip_ref, out_ref, scores_ref,
):
    rows = pre_ref.shape[0]
    half_rows = rows // 2
    channels = pre_ref.shape[1]
    half = channels // 2
    acceptor = own_ref[...]
    numbers = lax.broadcasted_iota(jnp.int32, (rows, half_rows), 0) + 1
    for ref in (low_ref, high_ref):
        asked = ref[half_rows:, :rows].astype(F32)[:1, :half_rows].astype(jnp.int32)
        acceptor = acceptor + mm(one_hot(numbers == asked), ref[:half_rows])
    acceptor = acceptor.astype(BF)
    product = product_ref[...]
    tracks = scores_ref.shape[0]
    scores_ref[:CHUNK] = mm(product, chunks_ref[6]).T.astype(BF)
    scores_ref[CHUNK:] = mm(product, chunks_ref[7]).T[: tracks - CHUNK].astype(BF)
    place = place_ref[...]
    grad = mm(split_hot(rows, True), fine_ref[...])
    for index in range(3):
        grad = grad + mm_nt(place[:, index * CHUNK : (index + 1) * CHUNK], chunks_ref[index])
        grad = grad + mm_nt(
            acceptor[:, index * CHUNK : (index + 1) * CHUNK], chunks_ref[3 + index]
        )
    pre = pre_ref[...]
    inv = inverse(pre)
    scaled = grad * gain_ref[:1]
    mean = jnp.mean(scaled * pre, -1, keepdims=True)
    skip = (inv * scaled - pre * (inv * inv * inv) * mean).astype(BF)
    skip_ref[...] = mm(split_hot(rows, False), skip).astype(BF)
    gains = jnp.sum(grad * pre * inv, 0, keepdims=True)
    row = lax.broadcasted_iota(jnp.int32, (half_rows, 128), 0)
    gain_block = jnp.zeros((half_rows, 128), F32)
    for index in range(channels // 128):
        gain_block = jnp.where(row == index, gains[:, index * 128 : (index + 1) * 128], gain_block)
    for index in range(8):
        start = half_rows if (index // 2) % 2 == 0 else 0
        part = (index % 2) * half
        out_ref[index, :, :half] = skip[start : start + half_rows, part : part + half]
        if index == 7:
            tracks = score_ref.shape[1]
            wide = jnp.zeros((rows, 2 * CHUNK - tracks), BF)
            block = jnp.concatenate([score_ref[:, CHUNK:], wide], 1)
        elif index == 6:
            block = score_ref[:, :CHUNK]
        elif index < 3:
            block = place_ref[:, index * CHUNK : (index + 1) * CHUNK]
        else:
            block = acceptor[:, (index - 3) * CHUNK : (index - 2) * CHUNK]
        out_ref[index, :, half : half + CHUNK] = block[:half_rows]
        out_ref[index, :, half + CHUNK :] = block[half_rows:]
    out_ref[7, :, half + 128 : half + CHUNK] = gain_block.astype(BF)


def partial_body(left_ref, near_ref, far_ref, grads_ref, out_ref, rows_ref, right_ref):
    x, c = lax.axis_index("x"), lax.axis_index("c")
    members, half_rows, _ = grads_ref.shape
    half = left_ref.shape[1] // 2
    rows = 2 * half_rows
    for member in range(members):
        span = pl.ds(member * rows, rows)
        step = lax.rem(x - member // 2 + 4, 4)

        @pl.when(c == member % 2)
        def _():
            rows_ref[span] = near_ref[step]

        @pl.when(c != member % 2)
        def _():
            rows_ref[span] = far_ref[step]

        right_ref[member * rows : member * rows + half_rows] = grads_ref[member, :, half : half + CHUNK]
        right_ref[member * rows + half_rows : (member + 1) * rows] = grads_ref[member, :, half + CHUNK :]
    taps = grads_ref[:, :, :half].reshape(members * half_rows, half)
    wide_y, wide_z, depth, _ = out_ref.shape

    def store(values, columns):
        for z in range(wide_z):
            for y in range(wide_y):
                row = (z * wide_y + y) * depth
                out_ref[y, z, :, columns] = values[row : row + depth].astype(BF)

    store(mm_tn(left_ref[...], taps), slice(0, half))
    rest = mm_tn(rows_ref[...], right_ref[...])
    total = jnp.sum(grads_ref[:, :16, half + 128 : half + CHUNK].astype(F32), 0)
    row = lax.broadcasted_iota(jnp.int32, (128, 128), 0)
    lane = lax.broadcasted_iota(jnp.int32, (128, 128), 1)
    ones = jnp.ones((128, 128), BF)
    gains = [
        mm(jnp.where(row == lane, total[index : index + 1], 0.0).astype(BF), ones)
        for index in range(2 * half // 128)
    ]
    store(rest[:, :128], slice(half, half + 128))
    gain_last = (x == 3) & (c == 1)
    store(
        jnp.where(gain_last, jnp.concatenate(gains, 0), rest[:, 128:]),
        slice(half + 128, half + CHUNK),
    )


def back_body(grads_ref, edge_ref, weight_ref, mine_ref, other_ref, rows_ref):
    x, c = lax.axis_index("x"), lax.axis_index("c")
    members, half_rows, _ = grads_ref.shape
    half = weight_ref.shape[1]
    shift_rows(x, 0, 3, lambda member: grads_ref[member, :, :half], edge_ref, rows_ref, members)
    result = mm_nt(rows_ref[...], weight_ref[...]).astype(BF)
    for member in range(members):
        block = result[member * half_rows : (member + 1) * half_rows]
        step = lax.rem(member // 2 - x + 4, 4)

        @pl.when(c == member % 2)
        def _():
            mine_ref[step] = block

        @pl.when(c != member % 2)
        def _():
            other_ref[step] = block


def add_body(left_ref, right_ref, out_ref):
    out_ref[...] = (left_ref[...].astype(F32) + right_ref[...].astype(F32)).astype(BF)


def copies_body(parts_ref, out_ref):
    total = parts_ref[0].astype(F32)
    for index in range(1, parts_ref.shape[0]):
        total = total + parts_ref[index].astype(F32)
    total = total.astype(BF)
    for index in range(out_ref.shape[0]):
        out_ref[index] = total


def final_body(
    rescale, shares_ref, backs_ref, conv_ref, donor_ref, acceptor_ref, track_ref, gain_ref, back_ref
):
    half = conv_ref.shape[2] // 2
    tracks = track_ref.shape[1]
    back = backs_ref[0].astype(F32)
    for member in range(1, backs_ref.shape[0]):
        back = back + backs_ref[member].astype(F32)
    back_ref[...] = back.astype(BF)
    for member in range(8):
        values = shares_ref[member].astype(F32) * rescale
        tap, part = member // 2, member % 2
        conv_ref[:, tap, part * half : (part + 1) * half] = values[:, :half]
        if member == 7:
            track_ref[:, CHUNK:] = values[:, half : half + tracks - CHUNK]
            depth = values.shape[0]
            column = values[:, half + CHUNK // 2 : half + CHUNK // 2 + 1]
            row = lax.broadcasted_iota(jnp.int32, (depth, depth), 0)
            lane = lax.broadcasted_iota(jnp.int32, (depth, depth), 1)
            gain_ref[...] = jnp.sum(jnp.where(row == lane, column, 0.0), 0, keepdims=True)
        else:
            target = (donor_ref, acceptor_ref, track_ref)[member // 3]
            first = (member % 3) * CHUNK
            target[:, first : first + CHUNK] = values[:, half : half + CHUNK]


def local(
    coarse,
    skip,
    donor,
    acceptor,
    conv_weight,
    donor_weight,
    acceptor_weight,
    track_weight,
    gain,
    fine_grad,
    score_grad,
):
    rows_in, _, channels = conv_weight.shape
    half_rows = coarse.shape[1]
    fine_rows = 2 * half_rows
    pairs = donor.shape[1]
    slots = pairs // 2
    tracks = track_weight.shape[1]
    half = channels // 2
    nz, ny, nx, nc = (lax.axis_size(axis) for axis in AXES)
    group_size = nx * nc
    seqs = nz * ny
    seq = lax.axis_index(SEQ)
    batch = lax.axis_index(GROUP)
    x, c = lax.axis_index("x"), lax.axis_index("c")

    both, own = call(
        start_body,
        [((nz, rows_in, half + CHUNK), BF), ((half_rows + 32, channels), BF)],
        conv_weight, donor_weight, acceptor_weight, track_weight, gain[None, :], coarse[0],
        mib=56,
    )
    both = lax.all_to_all(both, "z", 0, 0, tiled=True)

    both = jnp.broadcast_to(both[None], (ny,) + both.shape)
    both = lax.all_to_all(both, "y", 0, 0, tiled=True)
    rest_mine = jnp.swapaxes(both[:, :, :, half:], 0, 1).reshape(channels, CHUNK)

    left_all = lax.all_gather(own, GROUP, axis=0)
    edge = jnp.where(x == 0, left_all[:, 0], left_all[:, half_rows - 1])
    edge = send_edge(edge, (-1, 0, 0, 1))
    tap_out, conv_w, left_rows = call(
        conv_body,
        [((group_size, half_rows, half), BF), ((channels, half), BF)]
        + [((group_size * half_rows, channels), BF)],
        both, left_all, edge,
    )
    rest_mine, tap_out = lax.optimization_barrier((rest_mine, tap_out))
    chunks = lax.all_gather(rest_mine, GROUP, axis=0)
    taps = lax.all_to_all(tap_out, GROUP, 0, 0, tiled=True)

    def split_place(place):
        return (place % 2) * half_rows + place // 2

    donor_place = split_place(donor[0] - seq * fine_rows)[:, None]
    owner = acceptor[0] // fine_rows
    group = owner - seq
    acceptor_place = split_place(acceptor[0] - owner * fine_rows)[:, None]

    fine_shape = (fine_rows, channels)
    sent_shape = (slots + 16, channels)
    pre_norm, unit = call(norm_body, [(fine_shape, F32), (fine_shape, BF)], taps, skip[0])
    near_high = send_seq(unit, -1)
    near_low = send_seq(unit, 1)
    hidden, product, to_low, to_high, place_donor, own_grads, gain_rows = call(
        pair_body,
        [(fine_shape, BF), (fine_shape, BF), (sent_shape, BF), (sent_shape, BF), (fine_shape, BF)]
        + [(fine_shape, F32), ((16, channels), F32)],
        pre_norm, chunks, near_low, near_high, donor_place, acceptor_place, group[:, None], group[None, :],
        score_grad[0],
        scratch=[pltpu.VMEM(fine_shape, BF), pltpu.VMEM(fine_shape, BF)],
    )
    grads_high = send_seq(to_low, -1)
    grads_low = send_seq(to_high, 1)
    is_track = [(x + step) % nx == nx - 1 for step in range(nx)]
    left_near = [jnp.where(last, product, hidden) for last in is_track]
    left_near = jnp.stack(
        left_near[:1] + [send_x(left_near[step], step) for step in range(1, nx)], 0
    )
    skip_out, outgoing, scores = call(
        skip_body,
        [(fine_shape, BF), ((group_size, half_rows, half + 2 * CHUNK), BF), ((tracks, pairs), BF)],
        product, fine_grad[0], own_grads, chunks, grads_low, grads_high, pre_norm, gain_rows, place_donor, score_grad[0],
    )
    left_far = swap_core(left_near)
    grads = lax.all_to_all(outgoing, GROUP, 0, 0, tiled=True)
    tap_grads = grads[:, :, :half]
    grad_edge = jnp.where(x == 0, tap_grads[:, half_rows - 1], tap_grads[:, 0])
    grad_edge = send_edge(grad_edge, (1, 0, 0, -1))
    (partials,) = call(
        partial_body,
        [((ny, nz, rows_in, half + CHUNK), BF)],
        left_rows, left_near, left_far, grads,
        scratch=[
            pltpu.VMEM((group_size * fine_rows, channels), BF),
            pltpu.VMEM((group_size * fine_rows, CHUNK), BF),
        ],
    )
    slabs = (nx, half_rows, channels)
    back_mine, back_other = call(
        back_body, [(slabs, BF), (slabs, BF)], grads, grad_edge, conv_w,
        scratch=[pltpu.VMEM((group_size * half_rows, half), BF)],
    )
    (back_sum,) = call(add_body, [(slabs, BF)], back_mine, swap_core(back_other))
    backs = jnp.stack(
        [back_sum[0]] + [send_x(back_sum[step], step) for step in range(1, nx)], 0
    )
    shares = lax.all_to_all(partials, "y", 0, 0, tiled=True)
    shares = jnp.sum(shares.astype(F32), 0).astype(BF)
    shares = lax.all_to_all(shares, "z", 0, 0, tiled=True)
    shares, backs = lax.optimization_barrier((shares, backs))
    (shares,) = call(copies_body, [((group_size, rows_in, half + CHUNK), BF)], shares)
    shares = lax.all_to_all(shares, GROUP, 0, 0, tiled=True)

    rescale = float(group_size * seqs * fine_rows) ** (-0.5)
    conv_grad, donor_grad, acceptor_grad, track_grad, gain_grad, coarse_back = call(
        functools.partial(final_body, rescale),
        [((rows_in, nx, channels), F32), ((rows_in, channels), F32), ((rows_in, channels), F32)]
        + [((rows_in, tracks), F32), ((1, rows_in), F32), ((half_rows, channels), BF)],
        shares, backs,
    )
    gain_grad = gain_grad[0]
    return (
        scores.T[None],
        coarse_back[None],
        skip_out[None],
        conv_grad,
        donor_grad,
        acceptor_grad,
        track_grad,
        gain_grad,
    )


def solution(mesh):
    wide = Mesh(mesh.devices.reshape(8, 4, 4, 2), AXES)
    return jax.shard_map(
        local,
        mesh=wide,
        in_specs=(
            P(GROUP, SEQ, None),
            P(GROUP, SEQ, None),
            P(GROUP, SEQ),
            P(GROUP, SEQ),
            P(SEQ, None, None),
            P(SEQ, None),
            P(SEQ, None),
            P(SEQ, None),
            P(SEQ),
            P(GROUP, SEQ, None),
            P(GROUP, SEQ, None),
        ),
        out_specs=(
            P(GROUP, SEQ, None),
            P(GROUP, SEQ, None),
            P(GROUP, SEQ, None),
            P(SEQ, None, None),
            P(SEQ, None),
            P(SEQ, None),
            P(SEQ, None),
            P(SEQ),
        ),
        check_vma=False,
    )
```
